256 devices in a mesh: leaf: 32 (over x, y, core), rhs: 8 (over z).
Axes of the slice: x: 4, y: 4, z: 8, core: 2. Of those that a mesh axis runs over, the one named last changes fastest.
Arguments:
- currents: bfloat16 [32, 1024, 256], P('rhs', 'leaf'), may hold values from -6 to 6
- counts: int32 [1024], P('leaf'), may hold values from 16 to 128, as said below
- neighbours: int32 [1024, 9], P('leaf'), may hold values from 0 to 1023, as said below
- source_maps: int32 [1024, 32], P('leaf'), may hold values from 0 to 127
- target_maps: int32 [1024, 1024], P(None, 'leaf'), may hold values from 0 to 127
- source_bases: bfloat16 [1024, 2, 128, 64], P('leaf'), may hold values from -0.375 to 0.375
- level_one: bfloat16 [128, 2, 64, 64], replicated, may hold values from -0.5 to 0.5
- level_two: bfloat16 [128, 2, 64, 64], replicated, may hold values from -0.015625 to 0.015625
- target_bases: bfloat16 [1024, 2, 128, 64], P('leaf'), may hold values from -0.5 to 0.5
- near_blocks: bfloat16 [1024, 9, 2, 128, 128], P('leaf', None, None, 'rhs'), may hold values from -0.125 to 0.125
Outputs:
- fields: float32 [32, 1024, 256], P('rhs', 'leaf')
The draws below stay inside these ranges and needn't reach their ends.
Inputs may be any that keep to these rules, and one draw needn't show every extreme that they name: `counts`: each box has at least 16 live unknowns; some box has exactly 128. `neighbours`: row t begins with t itself; its other entries are distinct boxes other than t, each at most 8 boxes away from t in box order.
All inputs are finite; a program needn't handle non-finite values.
Results may differ from the reference program's by a relative error of at most 0.0029.
Values may be sent and summed in bfloat16 or wider, within the bound.
No kernel may reach another device: no remote copies, remote signals or barrier semaphores. Data moves between devices by JAX's collectives and lax.ppermute only.
A program may use at most 128 MiB of HBM per device.

```python
import jax
import jax.numpy as jnp
from jax import lax

P_SIZE = 128
R = 64
K = 128
NB = 9
SPAN = 8
BOX_DEV = 32
ANG = 32
BOXES = 1024
GROUPS = 32


def draw_counts(key, part):
    key = jax.random.fold_in(key, 11)
    first, second, third = jax.random.split(key, 3)
    values = jax.random.randint(first, (BOXES,), P_SIZE // 8, P_SIZE + 1)
    top_place = jax.random.randint(second, (), 0, BOXES)
    low_place = (top_place + 1 + jax.random.randint(third, (), 0, BOXES - 1)) % BOXES
    values = values.at[top_place].set(P_SIZE)
    values = values.at[low_place].set(P_SIZE // 8)
    return values.astype(jnp.int32)


def draw_neighbours(key, part):
    key = jax.random.fold_in(key, 23)
    rows = jnp.arange(BOXES, dtype=jnp.int32)[:, None]
    column = jnp.arange(2 * SPAN, dtype=jnp.int32)
    offsets = jnp.where(column < SPAN, column - SPAN, column - SPAN + 1)
    candidates = rows + offsets[None, :]
    valid = (candidates >= 0) & (candidates < BOXES)
    scores = jax.random.randint(key, (BOXES, 2 * SPAN), 0, 2 ** 20) * 64 + column[None, :]
    scores = jnp.where(valid, scores, -1 - column[None, :])
    best_values, best_places = jax.lax.top_k(scores, NB - 1)
    chosen = jnp.take_along_axis(candidates, best_places, axis=1)
    return jnp.concatenate([rows, chosen], axis=1).astype(jnp.int32)


def touch_ends(drawn, key, smallest, top_value):
    shape = drawn.shape
    place = [jax.random.randint(jax.random.fold_in(key, axis), (), 0, shape[axis]) for axis in range(len(shape))]
    drawn = drawn.at[tuple(place)].set(smallest)
    longest = shape.index(max(shape))
    place[longest] = (place[longest] + 1) % shape[longest]
    return drawn.at[tuple(place)].set(top_value)


def shard_levels(key, dims, shards, least, high):
    def one(axis_at, blocks):
        steps = jax.random.uniform(jax.random.fold_in(jax.random.fold_in(key, 6), axis_at), (blocks,), jnp.float32, least / len(shards), high / len(shards))
        return jnp.repeat(jnp.exp(steps), dims[axis_at] // blocks).reshape((-1,) + (1,) * (len(dims) - axis_at - 1))

    loudness = one(*shards[0])
    for cut in shards[1:]:
        loudness = loudness * one(*cut)
    return loudness


def centred(rng, dims, scale, most, cuts=(), kind=jnp.bfloat16):
    array = jax.random.normal(rng, dims, jnp.float32) * scale
    if len(cuts) > 0:
        array = shard_levels(rng, dims, cuts, -0.22, 0.18) * array
    return jnp.clip(array, min=-most, max=most).astype(kind)


def setup_inputs(seed: int = 0) -> dict:
    key_of = jax.random.split(jax.random.key(seed), 11)
    return {
        "currents": centred(key_of[0], (ANG, BOXES, 2 * P_SIZE), 1.0, 6.0, ((0, 8), (1, 32))),
        "counts": draw_counts(jax.random.fold_in(key_of[10], 71), 0),
        "neighbours": draw_neighbours(jax.random.fold_in(key_of[10], 71), 0),
        "source_maps": touch_ends(jax.random.randint(key_of[3], (BOXES, GROUPS), 0, K), jax.random.fold_in(key_of[3], 1), 0, K - 1).astype(jnp.int32),
        "target_maps": touch_ends(jax.random.randint(key_of[4], (BOXES, BOXES), 0, K), jax.random.fold_in(key_of[4], 1), 0, K - 1).astype(jnp.int32),
        "source_bases": centred(key_of[5], (BOXES, 2, P_SIZE, R), (2 * P_SIZE) ** -0.5, 0.375, ((0, 32),)),
        "level_one": centred(key_of[6], (K, 2, R, R), (2 * R) ** -0.5, 0.5),
        "level_two": centred(key_of[7], (K, 2, R, R), (2 * R * BOXES) ** -0.5, 0.015625),
        "target_bases": centred(key_of[8], (BOXES, 2, P_SIZE, R), (2 * R) ** -0.5, 0.5, ((0, 32),)),
        "near_blocks": centred(key_of[9], (BOXES, NB, 2, P_SIZE, P_SIZE), (2 * P_SIZE * NB) ** -0.5, 0.125, ((0, 32), (3, 8))),
    }


def combine(x):
    return jnp.stack([x[..., 0, 0, :] - x[..., 1, 1, :], x[..., 0, 1, :] + x[..., 1, 0, :]], -2)


def reference(currents, counts, neighbours, source_maps, target_maps, source_bases, level_one, level_two, target_bases, near_blocks):
    high = lax.Precision.HIGHEST
    live = (jnp.arange(P_SIZE)[None, :] < counts[:, None])
    blocks = near_blocks.astype(jnp.float32)
    bases_in = source_bases.astype(jnp.float32)
    kernels_one = level_one.astype(jnp.float32)
    kernels_two = level_two.astype(jnp.float32)
    bases_out = target_bases.astype(jnp.float32)
    groups = (jnp.arange(BOXES) // BOX_DEV).astype(jnp.int32)
    segment_ids = target_maps + K * jnp.arange(BOXES, dtype=jnp.int32)[None, :]

    def one_angle(current):
        masked = current.reshape(BOXES, 2, P_SIZE) * live[:, None, :].astype(jnp.bfloat16)
        masked_f = masked.astype(jnp.float32)
        picked = masked_f[neighbours]
        near_raw = jnp.einsum('tncp,tndqp->tcdq', picked, blocks, precision=high)
        near = jnp.stack([near_raw[:, 0, 0] - near_raw[:, 1, 1], near_raw[:, 0, 1] + near_raw[:, 1, 0]], 1)
        coef_raw = jnp.einsum('bcp,bdpr->bcdr', masked_f, bases_in, precision=high)
        coef = combine(coef_raw).astype(jnp.bfloat16)
        lifted = jnp.einsum('bcr,kdrs->bkcds', coef.astype(jnp.float32), kernels_one, precision=high)
        every_kernel = combine(lifted).reshape(BOXES, K, 2 * R)
        pieces = jnp.take_along_axis(every_kernel, source_maps[:, :, None], axis=1).astype(jnp.bfloat16)
        arrived = pieces[:, groups, :].astype(jnp.float32)
        summed = jax.ops.segment_sum(arrived.reshape(BOXES * BOXES, 2 * R), segment_ids.reshape(-1), num_segments=BOXES * K)
        summed = summed.reshape(BOXES, K, 2, R)
        far_coef = combine(jnp.einsum('tkcr,kdrs->tcds', summed, kernels_two, precision=high))
        far = combine(jnp.einsum('tcr,tdqr->tcdq', far_coef, bases_out, precision=high))
        total = (near + far) * live[:, None, :].astype(jnp.float32)
        return total.reshape(BOXES, 2 * P_SIZE)

    return lax.map(one_angle, currents)
```

```python
import jax
import jax.numpy as jnp
from jax import lax
from jax.experimental import pallas as pl
from jax.experimental.pallas import tpu as pltpu
from jax.sharding import PartitionSpec as P

SPAN = 8
PITCH = 129
F32 = jnp.float32
BF16 = jnp.bfloat16
VMEM = pl.BlockSpec(memory_space=pltpu.VMEM)
SMEM = pl.BlockSpec(memory_space=pltpu.SMEM)
NT = (((1,), (1,)), ((), ()))


def params(mib):
    return pltpu.CompilerParams(vmem_limit_bytes=mib * 2**20)


def live_lanes(counts_ref, boxes, points):
    row = lax.broadcasted_iota(jnp.int32, (boxes, points), 0)
    limit = jnp.zeros((boxes, points), jnp.int32)
    for box in range(boxes):
        limit = jnp.where(row == box, counts_ref[box], limit)
    lane = lax.broadcasted_iota(jnp.int32, (boxes, points), 1)
    return lane < limit


def mask_kernel(counts_ref, currents_ref, masked_ref, copies_ref):
    angles, boxes, doubled = currents_ref.shape
    points = doubled // 2
    live = live_lanes(counts_ref, boxes, points)
    for a in range(angles):
        for c in range(2):
            lanes = slice(c * points, (c + 1) * points)
            kept = jnp.where(live, currents_ref[a, :, lanes].astype(F32), 0.0).astype(BF16)
            masked_ref[a, :, lanes] = kept
            for z in range(copies_ref.shape[0]):
                copies_ref[z, a, :, lanes] = kept


def beside(*parts):
    return jnp.concatenate(parts, axis=1)


def above(*parts):
    return jnp.concatenate(parts, axis=0)


def turn_kernels(kernels_ref, turned):
    _, rank, _, kernel_count = kernels_ref.shape

    def one(r, _):
        real, imag = kernels_ref[0, r], kernels_ref[1, r]
        turned[pl.ds(r, kernel_count, stride=PITCH), :] = above(real, imag).T.astype(F32)
        turned[pl.ds(rank + r, kernel_count, stride=PITCH), :] = above(-imag, real).T.astype(F32)
        return 0

    lax.fori_loop(0, rank, one, 0, unroll=4)


def lift_kernel(maps_ref, masked_ref, bases_ref, kernels_ref, out_ref, rows, raws, turned, lifted, staged):
    angles, boxes, doubled = masked_ref.shape
    points = doubled // 2
    _, rank, _, kernel_count = kernels_ref.shape
    groups = out_ref.shape[0]
    wide = 2 * rank
    each = 2 * angles
    for a in range(angles):
        for c in range(2):
            rows[pl.ds(c * angles + a, boxes, stride=each), :] = masked_ref[
                a, :, c * points : (c + 1) * points
            ].astype(F32)
    for box in range(boxes):
        x = rows[each * box : each * (box + 1), :].astype(BF16)
        raws[each * box : each * (box + 1), :] = lax.dot_general(
            x, above(bases_ref[box, 0], bases_ref[box, 1]), NT, preferred_element_type=F32
        )
    raw = raws[...].reshape(boxes, 2, angles, wide)
    crossed = pltpu.roll(raw[:, 1].reshape(boxes * angles, wide), rank, 1)
    lane = lax.broadcasted_iota(jnp.int32, crossed.shape, 1)
    straight = raw[:, 0].reshape(boxes * angles, wide)
    coef = (straight + jnp.where(lane < rank, -crossed, crossed)).astype(BF16)
    turn_kernels(kernels_ref, turned)

    def pair(step, _):
        k = 2 * step
        weights = beside(turned[pl.ds(k * PITCH, wide), :], turned[pl.ds((k + 1) * PITCH, wide), :])
        both = jnp.dot(coef, weights.astype(BF16), preferred_element_type=F32)
        lifted[k] = both[:, :wide]
        lifted[k + 1] = both[:, wide:]
        return 0

    lax.fori_loop(0, kernel_count // 2, pair, 0, unroll=16)
    pitch = boxes + 1

    def one_group(g, slot):
        for box in range(boxes):
            k = maps_ref[box, g]
            staged[slot, pl.ds(box, angles, stride=pitch), :] = lifted[
                k, angles * box : angles * (box + 1), :
            ]
        for a in range(angles):
            out_ref[g, :, a * wide : (a + 1) * wide] = staged[
                slot, a * pitch : a * pitch + boxes, :
            ].astype(BF16)

    def two_groups(step, _):
        one_group(2 * step, 0)
        one_group(2 * step + 1, 1)
        return 0

    lax.fori_loop(0, groups // 2, two_groups, 0)


def pack_kernel(every_ref, out_ref, head_ref, tail_ref, spread):
    parts, angles, boxes, doubled = every_ref.shape
    points = doubled // 2
    total = parts * angles
    pitch = total + 1
    for z in range(parts):
        for a in range(angles):
            for c in range(2):
                spread[c, pl.ds(a * parts + z, boxes, stride=pitch), :] = every_ref[
                    z, a, :, c * points : (c + 1) * points
                ].astype(F32)
    for box in range(boxes):
        for c in range(2):
            lanes = slice(c * points, (c + 1) * points)
            rows = spread[c, box * pitch : box * pitch + total, :].astype(BF16)
            out_ref[box, :, lanes] = rows
            if box < SPAN:
                head_ref[box, :, lanes] = rows
            if box >= boxes - SPAN:
                tail_ref[box - (boxes - SPAN), :, lanes] = rows


def near_rows(sources, ids, blocks_ref, t, total, angles):
    nearby, _, owned, points = blocks_ref.shape[1:]
    parts = total // angles
    held, weights = [], []
    for n in range(nearby):
        held.append(sources[ids[n]])
        real, imag = blocks_ref[t, n, 0], blocks_ref[t, n, 1]
        weights.append(above(beside(real, -imag), beside(imag, real)))
    summed = lax.dot_general(beside(*held), beside(*weights), NT, preferred_element_type=F32)
    return beside(*[summed[a * parts : (a + 1) * parts] for a in range(angles)])


def inner_kernel(neighbours_ref, own_ref, blocks_ref, out_ref, rows):
    boxes, total, _ = own_ref.shape
    parts, inner, lanes = out_ref.shape
    angles = total // parts
    pitch = inner + 1

    def target(step, _):
        t = SPAN + step
        ids = [t + neighbours_ref[n, t] - neighbours_ref[0, t] for n in range(blocks_ref.shape[1])]
        rows[pl.ds(step, parts, stride=pitch), :] = near_rows(own_ref, ids, blocks_ref, t, total, angles)
        return 0

    lax.fori_loop(0, inner, target, 0, unroll=4)
    for z in range(parts):
        out_ref[z] = rows[z * pitch : z * pitch + inner, :].astype(BF16)


def outer_kernel(neighbours_ref, own_ref, before_ref, after_ref, inner_ref, blocks_ref, out_ref, window, rows):
    boxes, total, _ = own_ref.shape
    parts, _, lanes = out_ref.shape
    angles = total // parts
    pitch = boxes + 1
    window[:SPAN] = before_ref[...]
    window[SPAN : 3 * SPAN] = own_ref[: 2 * SPAN]
    window[3 * SPAN : 5 * SPAN] = own_ref[boxes - 2 * SPAN :]
    window[5 * SPAN :] = after_ref[...]

    def target(step, _):
        late = step // SPAN
        t = step + late * (boxes - 2 * SPAN)
        base = step + SPAN + late * 2 * SPAN - neighbours_ref[0, t]
        ids = [base + neighbours_ref[n, t] for n in range(blocks_ref.shape[1])]
        rows[pl.ds(t, parts, stride=pitch), :] = near_rows(window, ids, blocks_ref, t, total, angles)
        return 0

    lax.fori_loop(0, 2 * SPAN, target, 0, unroll=4)
    for z in range(parts):
        out_ref[z, :SPAN] = rows[z * pitch : z * pitch + SPAN, :].astype(BF16)
        out_ref[z, SPAN : boxes - SPAN] = inner_ref[z]
        out_ref[z, boxes - SPAN :] = rows[z * pitch + boxes - SPAN : z * pitch + boxes, :].astype(BF16)


CHUNK = 32


def far_kernel(maps_ref, pieces_ref, kernels_ref, bases_ref, out_ref, table, turned, total_ref):
    sources, lanes = pieces_ref.shape
    _, rank, _, kernel_count = kernels_ref.shape
    boxes, _, _, points = bases_ref.shape
    wide = 2 * rank
    angles = lanes // wide
    turn_kernels(kernels_ref, turned)
    table[...] = maps_ref[...].astype(F32).astype(BF16)
    total_ref[...] = jnp.zeros_like(total_ref)
    one, zero = jnp.ones((), BF16), jnp.zeros((), BF16)

    def chunk(step, _):
        first = step * CHUNK
        maps = table[...]
        chosen = above(*[jnp.where(maps == (first + i).astype(BF16), one, zero) for i in range(CHUNK)])
        summed = jnp.dot(chosen, pieces_ref[...], preferred_element_type=F32)
        xs, weights = [], []
        for i in range(CHUNK):
            x = above(
                *[summed[i * boxes : (i + 1) * boxes, a * wide : (a + 1) * wide] for a in range(angles)]
            )
            w = turned[pl.ds((first + i) * PITCH, wide), :].astype(BF16)
            high = x.astype(BF16)
            xs += [high, (x - high.astype(F32)).astype(BF16)]
            weights += [w, w]
        total_ref[...] += jnp.dot(beside(*xs), above(*weights), preferred_element_type=F32)
        return 0

    lax.fori_loop(0, kernel_count // CHUNK, chunk, 0)
    for t in range(boxes):
        x = total_ref[pl.ds(t, angles, stride=boxes), :]
        high = x.astype(BF16).astype(F32)
        both = above(high, x - high).astype(BF16)
        real, imag = bases_ref[t, 0], bases_ref[t, 1]
        weights = beside(above(real, -imag), above(imag, real))
        far = jnp.dot(both, weights, preferred_element_type=F32)
        far = far[:angles] + far[angles:]
        for c in range(2):
            out_ref[c, pl.ds(t, angles, stride=boxes), :] = far[:, c * points : (c + 1) * points]


def finish_kernel(counts_ref, near_ref, far_ref, out_ref):
    parts, boxes, lanes = near_ref.shape
    angles, _, doubled = out_ref.shape
    points = doubled // 2
    owned = points // parts
    live = live_lanes(counts_ref, boxes, points)
    block = lax.broadcasted_iota(jnp.int32, (boxes, points), 1) // owned
    near = [near_ref[z].astype(F32) for z in range(parts)]
    for a in range(angles):
        for c in range(2):
            place = (a * 2 + c) * owned
            joined = jnp.zeros((boxes, points), F32)
            for z in range(parts):
                shift = (z * owned - place) % lanes
                moved = near[z] if shift == 0 else pltpu.roll(near[z], shift, 1)
                joined = jnp.where(block == z, moved, joined)
            lanes_out = slice(c * points, (c + 1) * points)
            far = far_ref[c, a * boxes : (a + 1) * boxes, :]
            out_ref[a, :, lanes_out] = jnp.where(live, joined + far, 0.0)


def shards(
    currents,
    counts,
    neighbours,
    source_maps,
    target_maps,
    source_bases,
    level_one,
    level_two,
    target_bases,
    near_blocks,
):
    angles, boxes, doubled = currents.shape
    points = doubled // 2
    kernel_count, _, rank, _ = level_one.shape
    wide = 2 * rank
    leaves, parts = lax.axis_size("leaf"), lax.axis_size("rhs")
    owned = near_blocks.shape[3]

    lines = lambda x: jnp.swapaxes(x, -1, -2)
    kernels_one = level_one.transpose(1, 2, 3, 0)
    kernels_two = level_two.transpose(1, 2, 3, 0)

    masked, copies = pl.pallas_call(
        mask_kernel,
        out_shape=(
            jax.ShapeDtypeStruct((angles, boxes, doubled), BF16),
            jax.ShapeDtypeStruct((parts, angles, boxes, doubled), BF16),
        ),
        in_specs=[SMEM, VMEM],
        out_specs=(VMEM, VMEM),
        name="mask",
    )(counts, currents)
    every = lax.all_to_all(copies, "rhs", split_axis=0, concat_axis=0, tiled=True)

    pieces = pl.pallas_call(
        lift_kernel,
        out_shape=jax.ShapeDtypeStruct((leaves, boxes, angles * wide), BF16),
        in_specs=[SMEM, VMEM, VMEM, VMEM],
        out_specs=VMEM,
        scratch_shapes=[
            pltpu.VMEM((boxes * 2 * angles, points), F32),
            pltpu.VMEM((boxes * 2 * angles, wide), F32),
            pltpu.VMEM((kernel_count * PITCH, wide), F32),
            pltpu.VMEM((kernel_count, boxes * angles, wide), F32),
            pltpu.VMEM((2, angles * (boxes + 1) + angles, wide), F32),
        ],
        compiler_params=params(32),
        cost_estimate=pl.CostEstimate(flops=2**33, bytes_accessed=8 * 2**20, transcendentals=0),
        name="lift",
    )(source_maps, masked, lines(source_bases), kernels_one)
    incoming = lax.all_to_all(pieces, "leaf", split_axis=0, concat_axis=0, tiled=True)

    total = parts * angles
    own, head, tail = pl.pallas_call(
        pack_kernel,
        out_shape=(
            jax.ShapeDtypeStruct((boxes, total, doubled), BF16),
            jax.ShapeDtypeStruct((SPAN, total, doubled), BF16),
            jax.ShapeDtypeStruct((SPAN, total, doubled), BF16),
        ),
        in_specs=[VMEM],
        out_specs=(VMEM, VMEM, VMEM),
        scratch_shapes=[pltpu.VMEM((2, boxes * (total + 1) + total, points), F32)],
        compiler_params=params(16),
        name="pack",
    )(every)
    before = lax.ppermute(tail, "leaf", [(i, (i + 1) % leaves) for i in range(leaves)])
    after = lax.ppermute(head, "leaf", [((i + 1) % leaves, i) for i in range(leaves)])

    near_ids = neighbours.T
    inner = boxes - 2 * SPAN
    inner_rows = pl.pallas_call(
        inner_kernel,
        out_shape=jax.ShapeDtypeStruct((parts, inner, angles * 2 * owned), BF16),
        in_specs=[SMEM, VMEM, VMEM],
        out_specs=VMEM,
        scratch_shapes=[pltpu.VMEM((parts * (inner + 1) + parts, angles * 2 * owned), F32)],
        compiler_params=params(16),
        cost_estimate=pl.CostEstimate(flops=2**31, bytes_accessed=2**21, transcendentals=0),
        name="inner",
    )(near_ids, own, near_blocks)
    rows = pl.pallas_call(
        outer_kernel,
        out_shape=jax.ShapeDtypeStruct((parts, boxes, angles * 2 * owned), BF16),
        in_specs=[SMEM] + [VMEM] * 5,
        out_specs=VMEM,
        scratch_shapes=[
            pltpu.VMEM((6 * SPAN, total, doubled), BF16),
            pltpu.VMEM((parts * (boxes + 1) + parts, angles * 2 * owned), F32),
        ],
        compiler_params=params(16),
        name="outer",
    )(near_ids, own, before, after, inner_rows, near_blocks)
    near = lax.all_to_all(rows, "rhs", split_axis=0, concat_axis=0, tiled=True)

    far = pl.pallas_call(
        far_kernel,
        out_shape=jax.ShapeDtypeStruct((2, angles * boxes, points), F32),
        in_specs=[VMEM, VMEM, VMEM, VMEM],
        out_specs=VMEM,
        scratch_shapes=[
            pltpu.VMEM((boxes, leaves * boxes), BF16),
            pltpu.VMEM((kernel_count * PITCH, wide), F32),
            pltpu.VMEM((angles * boxes, wide), F32),
        ],
        compiler_params=params(40),
        cost_estimate=pl.CostEstimate(flops=2**33, bytes_accessed=8 * 2**20, transcendentals=0),
        name="far",
    )(target_maps.T, incoming.reshape(leaves * boxes, angles * wide), kernels_two, lines(target_bases))

    return pl.pallas_call(
        finish_kernel,
        out_shape=jax.ShapeDtypeStruct((angles, boxes, doubled), F32),
        in_specs=[SMEM, VMEM, VMEM],
        out_specs=VMEM,
        name="finish",
    )(counts, near, far)


def solution(mesh):
    placed = (
        P("rhs", "leaf", None),
        P("leaf"),
        P("leaf", None),
        P("leaf", None),
        P(None, "leaf"),
        P("leaf", None, None, None),
        P(),
        P(),
        P("leaf", None, None, None),
        P("leaf", None, None, "rhs", None),
    )
    return jax.shard_map(
        shards, mesh=mesh, in_specs=placed, out_specs=P("rhs", "leaf", None), check_vma=False
    )
```

```python
import jax
import jax.numpy as jnp
from jax import lax
from jax.experimental import pallas as pl
from jax.experimental.pallas import tpu as pltpu
from jax.sharding import PartitionSpec as P

SPAN = 8
PITCH = 129
F32 = jnp.float32
BF16 = jnp.bfloat16
VMEM = pl.BlockSpec(memory_space=pltpu.VMEM)
SMEM = pl.BlockSpec(memory_space=pltpu.SMEM)
ANY = pl.BlockSpec(memory_space=pl.ANY)
NT = (((1,), (1,)), ((), ()))


def params(mib):
    return pltpu.CompilerParams(vmem_limit_bytes=mib * 2**20)


def live_lanes(counts_ref, boxes, points):
    row = lax.broadcasted_iota(jnp.int32, (boxes, points), 0)
    limit = jnp.zeros((boxes, points), jnp.int32)
    for box in range(boxes):
        limit = jnp.where(row == box, counts_ref[box], limit)
    lane = lax.broadcasted_iota(jnp.int32, (boxes, points), 1)
    return lane < limit


def mask_kernel(counts_ref, currents_ref, masked_ref):
    angles, boxes, doubled = currents_ref.shape
    points = doubled // 2
    live = live_lanes(counts_ref, boxes, points)
    for a in range(angles):
        for c in range(2):
            lanes = slice(c * points, (c + 1) * points)
            kept = jnp.where(live, currents_ref[a, :, lanes].astype(F32), 0.0).astype(BF16)
            masked_ref[a, :, lanes] = kept


def beside(*parts):
    return jnp.concatenate(parts, axis=1)


def above(*parts):
    return jnp.concatenate(parts, axis=0)


def turn_kernels(kernels_ref, turned):
    _, rank, _, kernel_count = kernels_ref.shape

    def one(r, _):
        real, imag = kernels_ref[0, r], kernels_ref[1, r]
        turned[pl.ds(r, kernel_count, stride=PITCH), :] = above(real, imag).T.astype(F32)
        turned[pl.ds(rank + r, kernel_count, stride=PITCH), :] = above(-imag, real).T.astype(F32)
        return 0

    lax.fori_loop(0, rank, one, 0, unroll=4)


def lift_kernel(
    maps_ref, masked_ref, bases_hbm, kernels_hbm, out_ref, bases_ref, kernels_ref, rows, raws, turned, lifted, staged, arrived
):
    load_bases = pltpu.make_async_copy(bases_hbm, bases_ref, arrived.at[0])
    load_kernels = pltpu.make_async_copy(kernels_hbm, kernels_ref, arrived.at[1])
    load_bases.start()
    load_kernels.start()
    angles, boxes, doubled = masked_ref.shape
    points = doubled // 2
    _, rank, _, kernel_count = kernels_ref.shape
    groups = out_ref.shape[0]
    wide = 2 * rank
    each = 2 * angles
    for a in range(angles):
        for c in range(2):
            rows[pl.ds(c * angles + a, boxes, stride=each), :] = masked_ref[
                a, :, c * points : (c + 1) * points
            ].astype(F32)
    load_bases.wait()
    for box in range(boxes):
        x = rows[each * box : each * (box + 1), :].astype(BF16)
        raws[each * box : each * (box + 1), :] = lax.dot_general(
            x, above(bases_ref[box, 0], bases_ref[box, 1]), NT, preferred_element_type=F32
        )
    raw = raws[...].reshape(boxes, 2, angles, wide)
    crossed = pltpu.roll(raw[:, 1].reshape(boxes * angles, wide), rank, 1)
    lane = lax.broadcasted_iota(jnp.int32, crossed.shape, 1)
    straight = raw[:, 0].reshape(boxes * angles, wide)
    coef = (straight + jnp.where(lane < rank, -crossed, crossed)).astype(BF16)
    load_kernels.wait()
    turn_kernels(kernels_ref, turned)

    def pair(step, _):
        k = 2 * step
        weights = beside(turned[pl.ds(k * PITCH, wide), :], turned[pl.ds((k + 1) * PITCH, wide), :])
        both = jnp.dot(coef, weights.astype(BF16), preferred_element_type=F32)
        lifted[k] = both[:, :wide]
        lifted[k + 1] = both[:, wide:]
        return 0

    lax.fori_loop(0, kernel_count // 2, pair, 0, unroll=16)
    pitch = boxes + 1

    def one_group(g, slot):
        for box in range(boxes):
            k = maps_ref[box, g]
            staged[slot, pl.ds(box, angles, stride=pitch), :] = lifted[
                k, angles * box : angles * (box + 1), :
            ]
        for a in range(angles):
            out_ref[g, :, a * wide : (a + 1) * wide] = staged[
                slot, a * pitch : a * pitch + boxes, :
            ].astype(BF16)

    def two_groups(step, _):
        one_group(2 * step, 0)
        one_group(2 * step + 1, 1)
        return 0

    lax.fori_loop(0, groups // 2, two_groups, 0)


def pack_kernel(*refs):
    every, (out_ref, head_ref, tail_ref, spread) = refs[:7], refs[-4:]
    angles, boxes, doubled = every[0].shape
    points = doubled // 2
    total = out_ref.shape[1]
    parts = total // angles
    pitch = total + 1
    me = lax.axis_index("rhs")
    back = 0
    for ref in every:
        for group in range(ref.shape[0] // angles):
            z = lax.rem(me + parts - back, parts)
            back += 1
            for a in range(angles):
                for c in range(2):
                    spread[c, pl.ds(a * parts + z, boxes, stride=pitch), :] = ref[
                        group * angles + a, :, c * points : (c + 1) * points
                    ].astype(F32)
    for box in range(boxes):
        for c in range(2):
            lanes = slice(c * points, (c + 1) * points)
            rows = spread[c, box * pitch : box * pitch + total, :].astype(BF16)
            out_ref[box, :, lanes] = rows
            if box < SPAN:
                head_ref[box, :, lanes] = rows
            if box >= boxes - SPAN:
                tail_ref[box - (boxes - SPAN), :, lanes] = rows


def near_rows(sources, ids, blocks_ref, t, total, angles):
    nearby, _, owned, points = blocks_ref.shape[1:]
    parts = total // angles
    held, weights = [], []
    for n in range(nearby):
        held.append(sources[ids[n]])
        real, imag = blocks_ref[t, n, 0], blocks_ref[t, n, 1]
        weights.append(above(beside(real, -imag), beside(imag, real)))
    summed = lax.dot_general(beside(*held), beside(*weights), NT, preferred_element_type=F32)
    return beside(*[summed[a * parts : (a + 1) * parts] for a in range(angles)])


def inner_kernel(neighbours_ref, own_ref, blocks_ref, out_ref, rows):
    boxes, total, _ = own_ref.shape
    parts, inner, lanes = out_ref.shape
    angles = total // parts
    pitch = inner + 1

    def target(step, _):
        t = SPAN + step
        ids = [t + neighbours_ref[n, t] - neighbours_ref[0, t] for n in range(blocks_ref.shape[1])]
        rows[pl.ds(step, parts, stride=pitch), :] = near_rows(own_ref, ids, blocks_ref, t, total, angles)
        return 0

    lax.fori_loop(0, inner, target, 0, unroll=4)
    for z in range(parts):
        out_ref[z] = rows[z * pitch : z * pitch + inner, :].astype(BF16)


def outer_kernel(neighbours_ref, own_ref, before_ref, after_ref, inner_ref, blocks_ref, out_ref, window, rows):
    boxes, total, _ = own_ref.shape
    parts, _, lanes = out_ref.shape
    angles = total // parts
    pitch = boxes + 1
    window[:SPAN] = before_ref[...]
    window[SPAN : 3 * SPAN] = own_ref[: 2 * SPAN]
    window[3 * SPAN : 5 * SPAN] = own_ref[boxes - 2 * SPAN :]
    window[5 * SPAN :] = after_ref[...]

    def target(step, _):
        late = step // SPAN
        t = step + late * (boxes - 2 * SPAN)
        base = step + SPAN + late * 2 * SPAN - neighbours_ref[0, t]
        ids = [base + neighbours_ref[n, t] for n in range(blocks_ref.shape[1])]
        rows[pl.ds(t, parts, stride=pitch), :] = near_rows(window, ids, blocks_ref, t, total, angles)
        return 0

    lax.fori_loop(0, 2 * SPAN, target, 0, unroll=4)
    for z in range(parts):
        out_ref[z, :SPAN] = rows[z * pitch : z * pitch + SPAN, :].astype(BF16)
        out_ref[z, SPAN : boxes - SPAN] = inner_ref[z]
        out_ref[z, boxes - SPAN :] = rows[z * pitch + boxes - SPAN : z * pitch + boxes, :].astype(BF16)


def turn_kernel(kernels_ref, out_ref, turned):
    turn_kernels(kernels_ref, turned)
    wide = out_ref.shape[1]

    def one(k, _):
        out_ref[k] = turned[pl.ds(k * PITCH, wide), :].astype(BF16)
        return 0

    lax.fori_loop(0, out_ref.shape[0], one, 0, unroll=8)


CHUNK = 32


def far_kernel(
    maps_ref, pieces_ref, kernels_hbm, bases_hbm, out_ref, table, kernels_ref, bases_ref, total_ref, arrived
):
    sources, lanes = pieces_ref.shape
    kernel_count, wide, _ = kernels_hbm.shape
    boxes, _, _, points = bases_hbm.shape
    angles = lanes // wide
    chunks = kernel_count // CHUNK

    def load_kernels(step):
        part = pl.ds(step * CHUNK, CHUNK)
        return pltpu.make_async_copy(kernels_hbm.at[part], kernels_ref.at[part], arrived.at[step])

    load_bases = pltpu.make_async_copy(bases_hbm, bases_ref, arrived.at[chunks])
    for step in range(chunks):
        load_kernels(step).start()
    load_bases.start()
    table[...] = maps_ref[...].astype(F32).astype(BF16)
    total_ref[...] = jnp.zeros_like(total_ref)
    one, zero = jnp.ones((), BF16), jnp.zeros((), BF16)

    def chunk(step, _):
        first = step * CHUNK
        maps = table[...]
        chosen = above(*[jnp.where(maps == (first + i).astype(BF16), one, zero) for i in range(CHUNK)])
        summed = jnp.dot(chosen, pieces_ref[...], preferred_element_type=F32)
        load_kernels(step).wait()
        xs, weights = [], []
        for i in range(CHUNK):
            x = above(
                *[summed[i * boxes : (i + 1) * boxes, a * wide : (a + 1) * wide] for a in range(angles)]
            )
            w = kernels_ref[first + i]
            high = x.astype(BF16)
            xs += [high, (x - high.astype(F32)).astype(BF16)]
            weights += [w, w]
        total_ref[...] += jnp.dot(beside(*xs), above(*weights), preferred_element_type=F32)
        return 0

    lax.fori_loop(0, chunks, chunk, 0)
    load_bases.wait()
    for t in range(boxes):
        x = total_ref[pl.ds(t, angles, stride=boxes), :]
        high = x.astype(BF16).astype(F32)
        both = above(high, x - high).astype(BF16)
        real, imag = bases_ref[t, 0], bases_ref[t, 1]
        weights = beside(above(real, -imag), above(imag, real))
        far = jnp.dot(both, weights, preferred_element_type=F32)
        far = far[:angles] + far[angles:]
        for c in range(2):
            out_ref[c, pl.ds(t, angles, stride=boxes), :] = far[:, c * points : (c + 1) * points]


def finish_kernel(counts_ref, near_ref, far_ref, out_ref):
    parts, boxes, lanes = near_ref.shape
    angles, _, doubled = out_ref.shape
    points = doubled // 2
    owned = points // parts
    live = live_lanes(counts_ref, boxes, points)
    block = lax.broadcasted_iota(jnp.int32, (boxes, points), 1) // owned
    near = [near_ref[z].astype(F32) for z in range(parts)]
    for a in range(angles):
        for c in range(2):
            place = (a * 2 + c) * owned
            joined = jnp.zeros((boxes, points), F32)
            for z in range(parts):
                shift = (z * owned - place) % lanes
                moved = near[z] if shift == 0 else pltpu.roll(near[z], shift, 1)
                joined = jnp.where(block == z, moved, joined)
            lanes_out = slice(c * points, (c + 1) * points)
            far = far_ref[c, a * boxes : (a + 1) * boxes, :]
            out_ref[a, :, lanes_out] = jnp.where(live, joined + far, 0.0)


def shards(
    currents,
    counts,
    neighbours,
    source_maps,
    target_maps,
    source_bases,
    level_one,
    level_two,
    target_bases,
    near_blocks,
):
    angles, boxes, doubled = currents.shape
    points = doubled // 2
    kernel_count, _, rank, _ = level_one.shape
    wide = 2 * rank
    leaves, parts = lax.axis_size("leaf"), lax.axis_size("rhs")
    owned = near_blocks.shape[3]

    lines = lambda x: jnp.swapaxes(x, -1, -2)
    kernels_one = level_one.transpose(1, 2, 3, 0)
    kernels_two = level_two.transpose(1, 2, 3, 0)

    masked = pl.pallas_call(
        mask_kernel,
        out_shape=jax.ShapeDtypeStruct((angles, boxes, doubled), BF16),
        in_specs=[SMEM, VMEM],
        out_specs=VMEM,
        compiler_params=params(60),
        name="mask",
    )(counts, currents)

    def passed(x, steps):
        return lax.ppermute(x, "rhs", [(i, (i + steps) % parts) for i in range(parts)])

    back1, ahead1 = passed(masked, 1), passed(masked, -1)
    back2, ahead2 = passed(masked, 2), passed(masked, -2)
    back34 = passed(jnp.concatenate([back1, back2], axis=0), 2)
    ahead3 = passed(ahead1, -2)
    every = (masked, back1, back2, back34, ahead3, ahead2, ahead1)

    pieces = pl.pallas_call(
        lift_kernel,
        out_shape=jax.ShapeDtypeStruct((leaves, boxes, angles * wide), BF16),
        in_specs=[SMEM, VMEM, ANY, ANY],
        out_specs=VMEM,
        scratch_shapes=[
            pltpu.VMEM((boxes, 2, rank, points), BF16),
            pltpu.VMEM((2, rank, rank, kernel_count), BF16),
            pltpu.VMEM((boxes * 2 * angles, points), F32),
            pltpu.VMEM((boxes * 2 * angles, wide), F32),
            pltpu.VMEM((kernel_count * PITCH, wide), F32),
            pltpu.VMEM((kernel_count, boxes * angles, wide), F32),
            pltpu.VMEM((2, angles * (boxes + 1) + angles, wide), F32),
            pltpu.SemaphoreType.DMA((2,)),
        ],
        compiler_params=params(60),
        cost_estimate=pl.CostEstimate(flops=2**33, bytes_accessed=8 * 2**20, transcendentals=0),
        name="lift",
    )(source_maps, masked, lines(source_bases), kernels_one)
    incoming = lax.all_to_all(pieces, "leaf", split_axis=0, concat_axis=0, tiled=True)

    total = parts * angles
    own, head, tail = pl.pallas_call(
        pack_kernel,
        out_shape=(
            jax.ShapeDtypeStruct((boxes, total, doubled), BF16),
            jax.ShapeDtypeStruct((SPAN, total, doubled), BF16),
            jax.ShapeDtypeStruct((SPAN, total, doubled), BF16),
        ),
        in_specs=[VMEM] * len(every),
        out_specs=(VMEM, VMEM, VMEM),
        scratch_shapes=[pltpu.VMEM((2, boxes * (total + 1) + total, points), F32)],
        compiler_params=params(6),
        name="pack",
    )(*every)
    before = lax.ppermute(tail, "leaf", [(i, (i + 1) % leaves) for i in range(leaves)])
    after = lax.ppermute(head, "leaf", [((i + 1) % leaves, i) for i in range(leaves)])

    near_ids = neighbours.T
    inner = boxes - 2 * SPAN
    inner_rows = pl.pallas_call(
        inner_kernel,
        out_shape=jax.ShapeDtypeStruct((parts, inner, angles * 2 * owned), BF16),
        in_specs=[SMEM, VMEM, VMEM],
        out_specs=VMEM,
        scratch_shapes=[pltpu.VMEM((parts * (inner + 1) + parts, angles * 2 * owned), F32)],
        compiler_params=params(4),
        cost_estimate=pl.CostEstimate(flops=2**31, bytes_accessed=2**21, transcendentals=0),
        name="inner",
    )(near_ids, own, near_blocks)
    rows = pl.pallas_call(
        outer_kernel,
        out_shape=jax.ShapeDtypeStruct((parts, boxes, angles * 2 * owned), BF16),
        in_specs=[SMEM] + [VMEM] * 5,
        out_specs=VMEM,
        scratch_shapes=[
            pltpu.VMEM((6 * SPAN, total, doubled), BF16),
            pltpu.VMEM((parts * (boxes + 1) + parts, angles * 2 * owned), F32),
        ],
        compiler_params=params(6),
        cost_estimate=pl.CostEstimate(flops=2**36, bytes_accessed=2**21, transcendentals=0),
        name="outer",
    )(near_ids, own, before, after, inner_rows, near_blocks)
    near = lax.all_to_all(rows, "rhs", split_axis=0, concat_axis=0, tiled=True)

    turned = pl.pallas_call(
        turn_kernel,
        out_shape=jax.ShapeDtypeStruct((kernel_count, wide, wide), BF16),
        in_specs=[VMEM],
        out_specs=VMEM,
        scratch_shapes=[pltpu.VMEM((kernel_count * PITCH, wide), F32)],
        compiler_params=params(60),
        cost_estimate=pl.CostEstimate(flops=2**31, bytes_accessed=6 * 2**20, transcendentals=0),
        name="turn",
    )(kernels_two)

    far = pl.pallas_call(
        far_kernel,
        out_shape=jax.ShapeDtypeStruct((2, angles * boxes, points), F32),
        in_specs=[VMEM, VMEM, ANY, ANY],
        out_specs=VMEM,
        scratch_shapes=[
            pltpu.VMEM((boxes, leaves * boxes), BF16),
            pltpu.VMEM((kernel_count, wide, wide), BF16),
            pltpu.VMEM((boxes, 2, rank, points), BF16),
            pltpu.VMEM((angles * boxes, wide), F32),
            pltpu.SemaphoreType.DMA((kernel_count // CHUNK + 1,)),
        ],
        compiler_params=params(60),
        cost_estimate=pl.CostEstimate(flops=2**33, bytes_accessed=8 * 2**20, transcendentals=0),
        name="far",
    )(target_maps.T, incoming.reshape(leaves * boxes, angles * wide), turned, lines(target_bases))

    return pl.pallas_call(
        finish_kernel,
        out_shape=jax.ShapeDtypeStruct((angles, boxes, doubled), F32),
        in_specs=[SMEM, VMEM, VMEM],
        out_specs=VMEM,
        compiler_params=params(4),
        name="finish",
    )(counts, near, far)


def solution(mesh):
    placed = (
        P("rhs", "leaf", None),
        P("leaf"),
        P("leaf", None),
        P("leaf", None),
        P(None, "leaf"),
        P("leaf", None, None, None),
        P(),
        P(),
        P("leaf", None, None, None),
        P("leaf", None, None, "rhs", None),
    )
    return jax.shard_map(
        shards, mesh=mesh, in_specs=placed, out_specs=P("rhs", "leaf", None), check_vma=False
    )
```

```python
import jax
import jax.numpy as jnp
from jax import lax
from jax.experimental import pallas as pl
from jax.experimental.pallas import tpu as pltpu
from jax.sharding import PartitionSpec as P

SPAN = 8
PITCH = 129
F32 = jnp.float32
BF16 = jnp.bfloat16
VMEM = pl.BlockSpec(memory_space=pltpu.VMEM)
SMEM = pl.BlockSpec(memory_space=pltpu.SMEM)
ANY = pl.BlockSpec(memory_space=pl.ANY)
NT = (((1,), (1,)), ((), ()))


def params(mib):
    return pltpu.CompilerParams(vmem_limit_bytes=mib * 2**20)


def live_lanes(counts_ref, boxes, points):
    row = lax.broadcasted_iota(jnp.int32, (boxes, points), 0)
    limit = jnp.zeros((boxes, points), jnp.int32)
    for box in range(boxes):
        limit = jnp.where(row == box, counts_ref[box], limit)
    lane = lax.broadcasted_iota(jnp.int32, (boxes, points), 1)
    return lane < limit


def mask_kernel(counts_ref, currents_ref, masked_ref):
    angles, boxes, doubled = currents_ref.shape
    points = doubled // 2
    live = live_lanes(counts_ref, boxes, points)
    for a in range(angles):
        for c in range(2):
            lanes = slice(c * points, (c + 1) * points)
            kept = jnp.where(live, currents_ref[a, :, lanes].astype(F32), 0.0).astype(BF16)
            masked_ref[a, :, lanes] = kept


def beside(*parts):
    return jnp.concatenate(parts, axis=1)


def above(*parts):
    return jnp.concatenate(parts, axis=0)


def turn_kernels(kernels_ref, turned):
    _, rank, _, kernel_count = kernels_ref.shape

    def one(r, _):
        real, imag = kernels_ref[0, r], kernels_ref[1, r]
        turned[pl.ds(r, kernel_count, stride=PITCH), :] = above(real, imag).T.astype(F32)
        turned[pl.ds(rank + r, kernel_count, stride=PITCH), :] = above(-imag, real).T.astype(F32)
        return 0

    lax.fori_loop(0, rank, one, 0, unroll=16)


def lift_kernel(
    maps_ref,
    masked_hbm,
    bases_hbm,
    kernels_hbm,
    out_hbm,
    masked_ref,
    bases_ref,
    kernels_ref,
    out_ref,
    rows,
    raws,
    turned,
    lifted,
    staged,
    arrived,
    sent,
):
    load_masked = pltpu.make_async_copy(masked_hbm, masked_ref, arrived.at[2])
    load_masked.start()
    load_bases = pltpu.make_async_copy(bases_hbm, bases_ref, arrived.at[0])
    load_kernels = pltpu.make_async_copy(kernels_hbm, kernels_ref, arrived.at[1])
    load_bases.start()
    load_kernels.start()
    load_masked.wait()
    angles, boxes, doubled = masked_ref.shape
    points = doubled // 2
    _, rank, _, kernel_count = kernels_ref.shape
    groups = out_ref.shape[0]
    wide = 2 * rank
    each = 2 * angles
    for a in range(angles):
        for c in range(2):
            rows[pl.ds(c * angles + a, boxes, stride=each), :] = masked_ref[
                a, :, c * points : (c + 1) * points
            ].astype(F32)
    load_bases.wait()
    for box in range(boxes):
        x = rows[each * box : each * (box + 1), :].astype(BF16)
        raws[each * box : each * (box + 1), :] = lax.dot_general(
            x, above(bases_ref[box, 0], bases_ref[box, 1]), NT, preferred_element_type=F32
        )
    raw = raws[...].reshape(boxes, 2, angles, wide)
    crossed = pltpu.roll(raw[:, 1].reshape(boxes * angles, wide), rank, 1)
    lane = lax.broadcasted_iota(jnp.int32, crossed.shape, 1)
    straight = raw[:, 0].reshape(boxes * angles, wide)
    coef = (straight + jnp.where(lane < rank, -crossed, crossed)).astype(BF16)
    load_kernels.wait()
    turn_kernels(kernels_ref, turned)

    def pair(step, _):
        k = 2 * step
        weights = beside(turned[pl.ds(k * PITCH, wide), :], turned[pl.ds((k + 1) * PITCH, wide), :])
        both = jnp.dot(coef, weights.astype(BF16), preferred_element_type=F32)
        lifted[k] = both[:, :wide]
        lifted[k + 1] = both[:, wide:]
        return 0

    lax.fori_loop(0, kernel_count // 2, pair, 0, unroll=True)
    pitch = boxes + 1

    def one_group(g, slot):
        for box in range(boxes):
            k = maps_ref[box, g]
            staged[slot, pl.ds(box, angles, stride=pitch), :] = lifted[
                k, angles * box : angles * (box + 1), :
            ]
        for a in range(angles):
            out_ref[g, :, a * wide : (a + 1) * wide] = staged[
                slot, a * pitch : a * pitch + boxes, :
            ].astype(BF16)

    def send(step):
        part = pl.ds(step * 4, 4)
        return pltpu.make_async_copy(out_ref.at[part], out_hbm.at[part], sent.at[step])

    def four_groups(step, _):
        for i in range(4):
            one_group(4 * step + i, i)
        send(step).start()
        return 0

    lax.fori_loop(0, groups // 4, four_groups, 0)
    for step in range(groups // 4):
        send(step).wait()


def pack_kernel(*refs):
    every, (out_ref, head_ref, tail_ref, spread) = refs[:7], refs[-4:]
    angles, boxes, doubled = every[0].shape
    points = doubled // 2
    total = out_ref.shape[1]
    parts = total // angles
    pitch = total + 1
    me = lax.axis_index("rhs")
    back = 0
    for ref in every:
        for group in range(ref.shape[0] // angles):
            z = lax.rem(me + parts - back, parts)
            back += 1
            for a in range(angles):
                for c in range(2):
                    spread[c, pl.ds(a * parts + z, boxes, stride=pitch), :] = ref[
                        group * angles + a, :, c * points : (c + 1) * points
                    ].astype(F32)
    for box in range(boxes):
        for c in range(2):
            lanes = slice(c * points, (c + 1) * points)
            rows = spread[c, box * pitch : box * pitch + total, :].astype(BF16)
            out_ref[box, :, lanes] = rows
            if box < SPAN:
                head_ref[box, :, lanes] = rows
            if box >= boxes - SPAN:
                tail_ref[box - (boxes - SPAN), :, lanes] = rows


def near_rows(sources, ids, blocks_ref, t, total, angles):
    nearby, _, owned, points = blocks_ref.shape[1:]
    parts = total // angles
    held, weights = [], []
    for n in range(nearby):
        held.append(sources[ids[n]])
        real, imag = blocks_ref[t, n, 0], blocks_ref[t, n, 1]
        weights.append(above(beside(real, -imag), beside(imag, real)))
    summed = lax.dot_general(beside(*held), beside(*weights), NT, preferred_element_type=F32)
    return beside(*[summed[a * parts : (a + 1) * parts] for a in range(angles)])


def inner_kernel(neighbours_ref, own_ref, blocks_ref, out_ref, rows):
    boxes, total, _ = own_ref.shape
    parts, inner, lanes = out_ref.shape
    angles = total // parts
    pitch = inner + 1

    def target(step, _):
        t = SPAN + step
        ids = [t + neighbours_ref[n, t] - neighbours_ref[0, t] for n in range(blocks_ref.shape[1])]
        rows[pl.ds(step, parts, stride=pitch), :] = near_rows(own_ref, ids, blocks_ref, t, total, angles)
        return 0

    lax.fori_loop(0, inner, target, 0, unroll=True)
    for z in range(parts):
        out_ref[z] = rows[z * pitch : z * pitch + inner, :].astype(BF16)


def outer_kernel(neighbours_ref, own_ref, before_ref, after_ref, inner_ref, blocks_ref, out_ref, window, rows):
    boxes, total, _ = own_ref.shape
    parts, _, lanes = out_ref.shape
    angles = total // parts
    pitch = boxes + 1
    window[:SPAN] = before_ref[...]
    window[SPAN : 3 * SPAN] = own_ref[: 2 * SPAN]
    window[3 * SPAN : 5 * SPAN] = own_ref[boxes - 2 * SPAN :]
    window[5 * SPAN :] = after_ref[...]

    def target(step, _):
        late = step // SPAN
        t = step + late * (boxes - 2 * SPAN)
        base = step + SPAN + late * 2 * SPAN - neighbours_ref[0, t]
        ids = [base + neighbours_ref[n, t] for n in range(blocks_ref.shape[1])]
        rows[pl.ds(t, parts, stride=pitch), :] = near_rows(window, ids, blocks_ref, t, total, angles)
        return 0

    lax.fori_loop(0, 2 * SPAN, target, 0, unroll=True)
    for z in range(parts):
        out_ref[z, :SPAN] = rows[z * pitch : z * pitch + SPAN, :].astype(BF16)
        out_ref[z, SPAN : boxes - SPAN] = inner_ref[z]
        out_ref[z, boxes - SPAN :] = rows[z * pitch + boxes - SPAN : z * pitch + boxes, :].astype(BF16)


def turn_kernel(kernels_ref, out_ref, turned):
    turn_kernels(kernels_ref, turned)
    wide = out_ref.shape[1]

    def one(k, _):
        out_ref[k] = turned[pl.ds(k * PITCH, wide), :].astype(BF16)
        return 0

    lax.fori_loop(0, out_ref.shape[0], one, 0, unroll=32)


CHUNK = 32


def far_kernel(
    maps_hbm,
    pieces_hbm,
    kernels_hbm,
    bases_hbm,
    out_ref,
    maps_ref,
    pieces_ref,
    kernels_ref,
    bases_ref,
    table,
    total_ref,
    arrived,
):
    sources, lanes = pieces_hbm.shape
    kernel_count, wide, _ = kernels_hbm.shape
    boxes, _, _, points = bases_hbm.shape
    angles = lanes // wide
    chunks = kernel_count // CHUNK

    def load_kernels(step):
        part = pl.ds(step * CHUNK, CHUNK)
        return pltpu.make_async_copy(kernels_hbm.at[part], kernels_ref.at[part], arrived.at[step])

    load_bases = pltpu.make_async_copy(bases_hbm, bases_ref, arrived.at[chunks])
    load_maps = pltpu.make_async_copy(maps_hbm, maps_ref, arrived.at[chunks + 1])
    load_pieces = pltpu.make_async_copy(pieces_hbm, pieces_ref, arrived.at[chunks + 2])
    load_maps.start()
    load_pieces.start()
    for step in range(chunks):
        load_kernels(step).start()
    load_bases.start()
    load_maps.wait()
    table[...] = maps_ref[...].astype(F32).astype(BF16)
    one, zero = jnp.ones((), BF16), jnp.zeros((), BF16)
    load_pieces.wait()
    total = None
    for step in range(chunks):
        first = step * CHUNK
        maps = table[...]
        chosen = above(*[jnp.where(maps == jnp.asarray(first + i, BF16), one, zero) for i in range(CHUNK)])
        summed = jnp.dot(chosen, pieces_ref[...], preferred_element_type=F32)
        load_kernels(step).wait()
        xs = [
            above(
                *[summed[i * boxes : (i + 1) * boxes, a * wide : (a + 1) * wide] for a in range(angles)]
            ).astype(BF16)
            for i in range(CHUNK)
        ]
        weights = kernels_ref[first : first + CHUNK].reshape(CHUNK * wide, wide)
        add = jnp.dot(beside(*xs), weights, preferred_element_type=F32)
        total = add if total is None else total + add
    total_ref[...] = total
    load_bases.wait()
    for t in range(boxes):
        x = total_ref[pl.ds(t, angles, stride=boxes), :]
        high = x.astype(BF16).astype(F32)
        both = above(high, x - high).astype(BF16)
        real, imag = bases_ref[t, 0], bases_ref[t, 1]
        weights = beside(above(real, -imag), above(imag, real))
        far = jnp.dot(both, weights, preferred_element_type=F32)
        far = far[:angles] + far[angles:]
        for c in range(2):
            out_ref[c, pl.ds(t, angles, stride=boxes), :] = far[:, c * points : (c + 1) * points]


def finish_kernel(counts_ref, near_ref, far_ref, out_ref):
    parts, boxes, lanes = near_ref.shape
    angles, _, doubled = out_ref.shape
    points = doubled // 2
    owned = points // parts
    live = live_lanes(counts_ref, boxes, points)
    block = lax.broadcasted_iota(jnp.int32, (boxes, points), 1) // owned
    near = [near_ref[z].astype(F32) for z in range(parts)]
    for a in range(angles):
        for c in range(2):
            place = (a * 2 + c) * owned
            joined = jnp.zeros((boxes, points), F32)
            for z in range(parts):
                shift = (z * owned - place) % lanes
                moved = near[z] if shift == 0 else pltpu.roll(near[z], shift, 1)
                joined = jnp.where(block == z, moved, joined)
            lanes_out = slice(c * points, (c + 1) * points)
            far = far_ref[c, a * boxes : (a + 1) * boxes, :]
            out_ref[a, :, lanes_out] = jnp.where(live, joined + far, 0.0)


def shards(
    currents,
    counts,
    neighbours,
    source_maps,
    target_maps,
    source_bases,
    level_one,
    level_two,
    target_bases,
    near_blocks,
):
    angles, boxes, doubled = currents.shape
    points = doubled // 2
    kernel_count, _, rank, _ = level_one.shape
    wide = 2 * rank
    leaves, parts = lax.axis_size("leaf"), lax.axis_size("rhs")
    owned = near_blocks.shape[3]

    lines = lambda x: jnp.swapaxes(x, -1, -2)
    kernels_one = level_one.transpose(1, 2, 3, 0)
    kernels_two = level_two.transpose(1, 2, 3, 0)

    masked = pl.pallas_call(
        mask_kernel,
        out_shape=jax.ShapeDtypeStruct((angles, boxes, doubled), BF16),
        in_specs=[SMEM, VMEM],
        out_specs=VMEM,
        compiler_params=params(60),
        name="mask",
    )(counts, currents)

    def passed(x, steps):
        return lax.ppermute(x, "rhs", [(i, (i + steps) % parts) for i in range(parts)])

    back1, ahead1 = passed(masked, 1), passed(masked, -1)
    back2, ahead2 = passed(masked, 2), passed(masked, -2)
    back34 = passed(jnp.concatenate([back1, back2], axis=0), 2)
    ahead3 = passed(ahead1, -2)
    every = (masked, back1, back2, back34, ahead3, ahead2, ahead1)

    pieces = pl.pallas_call(
        lift_kernel,
        out_shape=jax.ShapeDtypeStruct((leaves, boxes, angles * wide), BF16),
        in_specs=[SMEM, ANY, ANY, ANY],
        out_specs=ANY,
        scratch_shapes=[
            pltpu.VMEM((angles, boxes, doubled), BF16),
            pltpu.VMEM((boxes, 2, rank, points), BF16),
            pltpu.VMEM((2, rank, rank, kernel_count), BF16),
            pltpu.VMEM((leaves, boxes, angles * wide), BF16),
            pltpu.VMEM((boxes * 2 * angles, points), F32),
            pltpu.VMEM((boxes * 2 * angles, wide), F32),
            pltpu.VMEM((kernel_count * PITCH, wide), F32),
            pltpu.VMEM((kernel_count, boxes * angles, wide), F32),
            pltpu.VMEM((4, angles * (boxes + 1) + angles, wide), F32),
            pltpu.SemaphoreType.DMA((3,)),
            pltpu.SemaphoreType.DMA((leaves // 4,)),
        ],
        compiler_params=params(60),
        cost_estimate=pl.CostEstimate(flops=2**33, bytes_accessed=8 * 2**20, transcendentals=0),
        name="lift",
    )(source_maps, masked, lines(source_bases), kernels_one)
    incoming = lax.all_to_all(pieces, "leaf", split_axis=0, concat_axis=0, tiled=True)

    total = parts * angles
    own, head, tail = pl.pallas_call(
        pack_kernel,
        out_shape=(
            jax.ShapeDtypeStruct((boxes, total, doubled), BF16),
            jax.ShapeDtypeStruct((SPAN, total, doubled), BF16),
            jax.ShapeDtypeStruct((SPAN, total, doubled), BF16),
        ),
        in_specs=[VMEM] * len(every),
        out_specs=(VMEM, VMEM, VMEM),
        scratch_shapes=[pltpu.VMEM((2, boxes * (total + 1) + total, points), F32)],
        compiler_params=params(6),
        name="pack",
    )(*every)
    before = lax.ppermute(tail, "leaf", [(i, (i + 1) % leaves) for i in range(leaves)])
    after = lax.ppermute(head, "leaf", [((i + 1) % leaves, i) for i in range(leaves)])

    near_ids = neighbours.T
    inner = boxes - 2 * SPAN
    inner_rows = pl.pallas_call(
        inner_kernel,
        out_shape=jax.ShapeDtypeStruct((parts, inner, angles * 2 * owned), BF16),
        in_specs=[SMEM, VMEM, VMEM],
        out_specs=VMEM,
        scratch_shapes=[pltpu.VMEM((parts * (inner + 1) + parts, angles * 2 * owned), F32)],
        compiler_params=params(4),
        cost_estimate=pl.CostEstimate(flops=2**31, bytes_accessed=2**21, transcendentals=0),
        name="inner",
    )(near_ids, own, near_blocks)
    rows = pl.pallas_call(
        outer_kernel,
        out_shape=jax.ShapeDtypeStruct((parts, boxes, angles * 2 * owned), BF16),
        in_specs=[SMEM] + [VMEM] * 5,
        out_specs=VMEM,
        scratch_shapes=[
            pltpu.VMEM((6 * SPAN, total, doubled), BF16),
            pltpu.VMEM((parts * (boxes + 1) + parts, angles * 2 * owned), F32),
        ],
        compiler_params=params(6),
        cost_estimate=pl.CostEstimate(flops=2**36, bytes_accessed=2**21, transcendentals=0),
        name="outer",
    )(near_ids, own, before, after, inner_rows, near_blocks)
    near = lax.all_to_all(rows, "rhs", split_axis=0, concat_axis=0, tiled=True)

    turned = pl.pallas_call(
        turn_kernel,
        out_shape=jax.ShapeDtypeStruct((kernel_count, wide, wide), BF16),
        in_specs=[VMEM],
        out_specs=VMEM,
        scratch_shapes=[pltpu.VMEM((kernel_count * PITCH, wide), F32)],
        compiler_params=params(12),
        cost_estimate=pl.CostEstimate(flops=2**31, bytes_accessed=6 * 2**20, transcendentals=0),
        name="turn",
    )(kernels_two)

    far = pl.pallas_call(
        far_kernel,
        out_shape=jax.ShapeDtypeStruct((2, angles * boxes, points), F32),
        in_specs=[ANY, ANY, ANY, ANY],
        out_specs=VMEM,
        scratch_shapes=[
            pltpu.VMEM((boxes, leaves * boxes), jnp.int32),
            pltpu.VMEM((leaves * boxes, angles * wide), BF16),
            pltpu.VMEM((kernel_count, wide, wide), BF16),
            pltpu.VMEM((boxes, 2, rank, points), BF16),
            pltpu.VMEM((boxes, leaves * boxes), BF16),
            pltpu.VMEM((angles * boxes, wide), F32),
            pltpu.SemaphoreType.DMA((kernel_count // CHUNK + 3,)),
        ],
        compiler_params=params(60),
        cost_estimate=pl.CostEstimate(flops=2**33, bytes_accessed=8 * 2**20, transcendentals=0),
        name="far",
    )(target_maps.T, incoming.reshape(leaves * boxes, angles * wide), turned, lines(target_bases))

    return pl.pallas_call(
        finish_kernel,
        out_shape=jax.ShapeDtypeStruct((angles, boxes, doubled), F32),
        in_specs=[SMEM, VMEM, VMEM],
        out_specs=VMEM,
        compiler_params=params(4),
        name="finish",
    )(counts, near, far)


def solution(mesh):
    placed = (
        P("rhs", "leaf", None),
        P("leaf"),
        P("leaf", None),
        P("leaf", None),
        P(None, "leaf"),
        P("leaf", None, None, None),
        P(),
        P(),
        P("leaf", None, None, None),
        P("leaf", None, None, "rhs", None),
    )
    return jax.shard_map(
        shards, mesh=mesh, in_specs=placed, out_specs=P("rhs", "leaf", None), check_vma=False
    )
```

```python
import jax
import jax.numpy as jnp
from jax import lax
from jax.experimental import pallas as pl
from jax.experimental.pallas import tpu as pltpu
from jax.sharding import PartitionSpec as P

SPAN = 8
PITCH = 129
F32 = jnp.float32
BF16 = jnp.bfloat16
VMEM = pl.BlockSpec(memory_space=pltpu.VMEM)
SMEM = pl.BlockSpec(memory_space=pltpu.SMEM)
ANY = pl.BlockSpec(memory_space=pl.ANY)
NT = (((1,), (1,)), ((), ()))


def params(mib):
    return pltpu.CompilerParams(vmem_limit_bytes=mib * 2**20)


def live_lanes(counts_ref, boxes, points):
    row = lax.broadcasted_iota(jnp.int32, (boxes, points), 0)
    limit = jnp.zeros((boxes, points), jnp.int32)
    for box in range(boxes):
        limit = jnp.where(row == box, counts_ref[box], limit)
    lane = lax.broadcasted_iota(jnp.int32, (boxes, points), 1)
    return lane < limit


def mask_kernel(counts_ref, currents_ref, masked_ref):
    angles, boxes, doubled = currents_ref.shape
    points = doubled // 2
    live = live_lanes(counts_ref, boxes, points)
    for a in range(angles):
        for c in range(2):
            lanes = slice(c * points, (c + 1) * points)
            kept = jnp.where(live, currents_ref[a, :, lanes].astype(F32), 0.0).astype(BF16)
            masked_ref[a, :, lanes] = kept


def beside(*parts):
    return jnp.concatenate(parts, axis=1)


def above(*parts):
    return jnp.concatenate(parts, axis=0)


def turn_kernels(kernels_ref, turned, first, count):
    _, rank, _, kernel_count = kernels_ref.shape

    def one(step, _):
        r = first + step
        real, imag = kernels_ref[0, r], kernels_ref[1, r]
        turned[pl.ds(r, kernel_count, stride=PITCH), :] = above(real, imag).T.astype(F32)
        turned[pl.ds(rank + r, kernel_count, stride=PITCH), :] = above(-imag, real).T.astype(F32)
        return 0

    lax.fori_loop(0, count, one, 0, unroll=16)


def lift_kernel(
    maps_hbm,
    masked_hbm,
    bases_hbm,
    kernels_hbm,
    out_hbm,
    maps_ref,
    masked_ref,
    bases_ref,
    kernels_ref,
    out_ref,
    rows,
    raws,
    turned,
    lifted,
    staged,
    arrived,
    sent,
):
    quarter = kernels_ref.shape[1] // 4

    def load_kernels(i):
        part = pl.ds(i * quarter, quarter)
        return pltpu.make_async_copy(kernels_hbm.at[:, part], kernels_ref.at[:, part], arrived.at[i])

    load_masked = pltpu.make_async_copy(masked_hbm, masked_ref, arrived.at[4])
    load_bases = pltpu.make_async_copy(bases_hbm, bases_ref, arrived.at[5])
    load_maps = pltpu.make_async_copy(maps_hbm, maps_ref, arrived.at[6])
    for i in range(4):
        load_kernels(i).start()
    load_masked.start()
    load_bases.start()
    load_maps.start()
    for i in range(4):
        load_kernels(i).wait()
        turn_kernels(kernels_ref, turned, i * quarter, quarter)
    load_masked.wait()
    angles, boxes, doubled = masked_ref.shape
    points = doubled // 2
    _, rank, _, kernel_count = kernels_ref.shape
    groups = out_ref.shape[0]
    wide = 2 * rank
    each = 2 * angles
    for a in range(angles):
        for c in range(2):
            rows[pl.ds(c * angles + a, boxes, stride=each), :] = masked_ref[
                a, :, c * points : (c + 1) * points
            ].astype(F32)
    load_bases.wait()
    for box in range(boxes):
        x = rows[each * box : each * (box + 1), :].astype(BF16)
        raws[each * box : each * (box + 1), :] = lax.dot_general(
            x, above(bases_ref[box, 0], bases_ref[box, 1]), NT, preferred_element_type=F32
        )
    raw = raws[...].reshape(boxes, 2, angles, wide)
    crossed = pltpu.roll(raw[:, 1].reshape(boxes * angles, wide), rank, 1)
    lane = lax.broadcasted_iota(jnp.int32, crossed.shape, 1)
    straight = raw[:, 0].reshape(boxes * angles, wide)
    coef = (straight + jnp.where(lane < rank, -crossed, crossed)).astype(BF16)

    def pair(step, _):
        k = 2 * step
        weights = beside(turned[pl.ds(k * PITCH, wide), :], turned[pl.ds((k + 1) * PITCH, wide), :])
        both = jnp.dot(coef, weights.astype(BF16), preferred_element_type=F32)
        lifted[k] = both[:, :wide]
        lifted[k + 1] = both[:, wide:]
        return 0

    lax.fori_loop(0, kernel_count // 2, pair, 0, unroll=True)
    pitch = boxes + 1
    load_maps.wait()

    def one_group(g, slot):
        for box in range(boxes):
            k = maps_ref[box, g]
            staged[slot, pl.ds(box, angles, stride=pitch), :] = lifted[
                k, angles * box : angles * (box + 1), :
            ]
        for a in range(angles):
            out_ref[g, :, a * wide : (a + 1) * wide] = staged[
                slot, a * pitch : a * pitch + boxes, :
            ].astype(BF16)

    def send(step):
        part = pl.ds(step * 4, 4)
        return pltpu.make_async_copy(out_ref.at[part], out_hbm.at[part], sent.at[step])

    def four_groups(step, _):
        for i in range(4):
            one_group(4 * step + i, i)
        send(step).start()
        return 0

    lax.fori_loop(0, groups // 4, four_groups, 0)
    for step in range(groups // 4):
        send(step).wait()


def pack_kernel(*refs):
    every, (out_ref, head_ref, tail_ref, spread) = refs[:7], refs[-4:]
    angles, boxes, doubled = every[0].shape
    points = doubled // 2
    total = out_ref.shape[1]
    parts = total // angles
    pitch = total + 1
    me = lax.axis_index("rhs")
    back = 0
    for ref in every:
        for group in range(ref.shape[0] // angles):
            z = lax.rem(me + parts - back, parts)
            back += 1
            for a in range(angles):
                for c in range(2):
                    spread[c, pl.ds(a * parts + z, boxes, stride=pitch), :] = ref[
                        group * angles + a, :, c * points : (c + 1) * points
                    ].astype(F32)
    for box in range(boxes):
        for c in range(2):
            lanes = slice(c * points, (c + 1) * points)
            rows = spread[c, box * pitch : box * pitch + total, :].astype(BF16)
            out_ref[box, :, lanes] = rows
            if box < SPAN:
                head_ref[box, :, lanes] = rows
            if box >= boxes - SPAN:
                tail_ref[box - (boxes - SPAN), :, lanes] = rows


def near_rows(sources, ids, blocks_ref, t, total, angles):
    nearby, _, owned, points = blocks_ref.shape[1:]
    parts = total // angles
    held, weights = [], []
    for n in range(nearby):
        held.append(sources[ids[n]])
        real, imag = blocks_ref[t, n, 0], blocks_ref[t, n, 1]
        weights.append(above(beside(real, -imag), beside(imag, real)))
    summed = lax.dot_general(beside(*held), beside(*weights), NT, preferred_element_type=F32)
    return beside(*[summed[a * parts : (a + 1) * parts] for a in range(angles)])


def inner_kernel(neighbours_ref, own_ref, blocks_ref, out_ref, rows):
    boxes, total, _ = own_ref.shape
    parts, inner, lanes = out_ref.shape
    angles = total // parts
    pitch = inner + 1

    def target(step, _):
        t = SPAN + step
        ids = [t + neighbours_ref[n, t] - neighbours_ref[0, t] for n in range(blocks_ref.shape[1])]
        rows[pl.ds(step, parts, stride=pitch), :] = near_rows(own_ref, ids, blocks_ref, t, total, angles)
        return 0

    lax.fori_loop(0, inner, target, 0, unroll=True)
    for z in range(parts):
        out_ref[z] = rows[z * pitch : z * pitch + inner, :].astype(BF16)


def outer_kernel(neighbours_ref, own_ref, before_ref, after_ref, inner_ref, blocks_ref, out_ref, window, rows):
    boxes, total, _ = own_ref.shape
    parts, _, lanes = out_ref.shape
    angles = total // parts
    pitch = boxes + 1
    window[:SPAN] = before_ref[...]
    window[SPAN : 3 * SPAN] = own_ref[: 2 * SPAN]
    window[3 * SPAN : 5 * SPAN] = own_ref[boxes - 2 * SPAN :]
    window[5 * SPAN :] = after_ref[...]

    def target(step, _):
        late = step // SPAN
        t = step + late * (boxes - 2 * SPAN)
        base = step + SPAN + late * 2 * SPAN - neighbours_ref[0, t]
        ids = [base + neighbours_ref[n, t] for n in range(blocks_ref.shape[1])]
        rows[pl.ds(t, parts, stride=pitch), :] = near_rows(window, ids, blocks_ref, t, total, angles)
        return 0

    lax.fori_loop(0, 2 * SPAN, target, 0, unroll=True)
    for z in range(parts):
        out_ref[z, :SPAN] = rows[z * pitch : z * pitch + SPAN, :].astype(BF16)
        out_ref[z, SPAN : boxes - SPAN] = inner_ref[z]
        out_ref[z, boxes - SPAN :] = rows[z * pitch + boxes - SPAN : z * pitch + boxes, :].astype(BF16)


def turn_kernel(kernels_ref, out_ref, turned):
    turn_kernels(kernels_ref, turned, 0, kernels_ref.shape[1])
    wide = out_ref.shape[1]

    def one(k, _):
        out_ref[k] = turned[pl.ds(k * PITCH, wide), :].astype(BF16)
        return 0

    lax.fori_loop(0, out_ref.shape[0], one, 0, unroll=32)


CHUNK = 32


def far_kernel(
    maps_hbm,
    pieces_hbm,
    kernels_hbm,
    bases_hbm,
    out_ref,
    maps_ref,
    pieces_ref,
    kernels_ref,
    bases_ref,
    table,
    total_ref,
    arrived,
):
    sources, lanes = pieces_hbm.shape
    kernel_count, wide, _ = kernels_hbm.shape
    boxes, _, _, points = bases_hbm.shape
    angles = lanes // wide
    chunks = kernel_count // CHUNK

    def load_kernels(step):
        part = pl.ds(step * CHUNK, CHUNK)
        return pltpu.make_async_copy(kernels_hbm.at[part], kernels_ref.at[part], arrived.at[step])

    load_bases = pltpu.make_async_copy(bases_hbm, bases_ref, arrived.at[chunks])
    load_maps = pltpu.make_async_copy(maps_hbm, maps_ref, arrived.at[chunks + 1])
    load_pieces = pltpu.make_async_copy(pieces_hbm, pieces_ref, arrived.at[chunks + 2])
    load_maps.start()
    load_pieces.start()
    for step in range(chunks):
        load_kernels(step).start()
    load_bases.start()
    load_maps.wait()
    table[...] = maps_ref[...].astype(F32).astype(BF16)
    one, zero = jnp.ones((), BF16), jnp.zeros((), BF16)
    load_pieces.wait()
    total = None
    for step in range(chunks):
        first = step * CHUNK
        maps = table[...]
        chosen = above(*[jnp.where(maps == jnp.asarray(first + i, BF16), one, zero) for i in range(CHUNK)])
        summed = jnp.dot(chosen, pieces_ref[...], preferred_element_type=F32)
        load_kernels(step).wait()
        xs = [
            above(
                *[summed[i * boxes : (i + 1) * boxes, a * wide : (a + 1) * wide] for a in range(angles)]
            ).astype(BF16)
            for i in range(CHUNK)
        ]
        weights = kernels_ref[first : first + CHUNK].reshape(CHUNK * wide, wide)
        add = jnp.dot(beside(*xs), weights, preferred_element_type=F32)
        total = add if total is None else total + add
    total_ref[...] = total
    load_bases.wait()
    for t in range(boxes):
        x = total_ref[pl.ds(t, angles, stride=boxes), :]
        high = x.astype(BF16).astype(F32)
        both = above(high, x - high).astype(BF16)
        real, imag = bases_ref[t, 0], bases_ref[t, 1]
        weights = beside(above(real, -imag), above(imag, real))
        far = jnp.dot(both, weights, preferred_element_type=F32)
        far = far[:angles] + far[angles:]
        for c in range(2):
            out_ref[c, pl.ds(t, angles, stride=boxes), :] = far[:, c * points : (c + 1) * points]


def finish_kernel(counts_ref, near_ref, far_ref, out_ref):
    parts, boxes, lanes = near_ref.shape
    angles, _, doubled = out_ref.shape
    points = doubled // 2
    owned = points // parts
    live = live_lanes(counts_ref, boxes, points)
    block = lax.broadcasted_iota(jnp.int32, (boxes, points), 1) // owned
    near = [near_ref[z].astype(F32) for z in range(parts)]
    for a in range(angles):
        for c in range(2):
            place = (a * 2 + c) * owned
            joined = jnp.zeros((boxes, points), F32)
            for z in range(parts):
                shift = (z * owned - place) % lanes
                moved = near[z] if shift == 0 else pltpu.roll(near[z], shift, 1)
                joined = jnp.where(block == z, moved, joined)
            lanes_out = slice(c * points, (c + 1) * points)
            far = far_ref[c, a * boxes : (a + 1) * boxes, :]
            out_ref[a, :, lanes_out] = jnp.where(live, joined + far, 0.0)


def shards(
    currents,
    counts,
    neighbours,
    source_maps,
    target_maps,
    source_bases,
    level_one,
    level_two,
    target_bases,
    near_blocks,
):
    angles, boxes, doubled = currents.shape
    points = doubled // 2
    kernel_count, _, rank, _ = level_one.shape
    wide = 2 * rank
    leaves, parts = lax.axis_size("leaf"), lax.axis_size("rhs")
    owned = near_blocks.shape[3]

    lines = lambda x: jnp.swapaxes(x, -1, -2)
    kernels_one = level_one.transpose(1, 2, 3, 0)
    kernels_two = level_two.transpose(1, 2, 3, 0)

    masked = pl.pallas_call(
        mask_kernel,
        out_shape=jax.ShapeDtypeStruct((angles, boxes, doubled), BF16),
        in_specs=[SMEM, VMEM],
        out_specs=VMEM,
        compiler_params=params(60),
        name="mask",
    )(counts, currents)

    def passed(x, steps):
        return lax.ppermute(x, "rhs", [(i, (i + steps) % parts) for i in range(parts)])

    back1, ahead1 = passed(masked, 1), passed(masked, -1)
    back2, ahead2 = passed(masked, 2), passed(masked, -2)
    back34 = passed(jnp.concatenate([back1, back2], axis=0), 2)
    ahead3 = passed(ahead1, -2)
    every = (masked, back1, back2, back34, ahead3, ahead2, ahead1)

    pieces = pl.pallas_call(
        lift_kernel,
        out_shape=jax.ShapeDtypeStruct((leaves, boxes, angles * wide), BF16),
        in_specs=[ANY, ANY, ANY, ANY],
        out_specs=ANY,
        scratch_shapes=[
            pltpu.SMEM((boxes, leaves), jnp.int32),
            pltpu.VMEM((angles, boxes, doubled), BF16),
            pltpu.VMEM((boxes, 2, rank, points), BF16),
            pltpu.VMEM((2, rank, rank, kernel_count), BF16),
            pltpu.VMEM((leaves, boxes, angles * wide), BF16),
            pltpu.VMEM((boxes * 2 * angles, points), F32),
            pltpu.VMEM((boxes * 2 * angles, wide), F32),
            pltpu.VMEM((kernel_count * PITCH, wide), F32),
            pltpu.VMEM((kernel_count, boxes * angles, wide), F32),
            pltpu.VMEM((4, angles * (boxes + 1) + angles, wide), F32),
            pltpu.SemaphoreType.DMA((7,)),
            pltpu.SemaphoreType.DMA((leaves // 4,)),
        ],
        compiler_params=params(60),
        cost_estimate=pl.CostEstimate(flops=2**33, bytes_accessed=8 * 2**20, transcendentals=0),
        name="lift",
    )(source_maps, masked, lines(source_bases), kernels_one)
    incoming = lax.all_to_all(pieces, "leaf", split_axis=0, concat_axis=0, tiled=True)

    total = parts * angles
    own, head, tail = pl.pallas_call(
        pack_kernel,
        out_shape=(
            jax.ShapeDtypeStruct((boxes, total, doubled), BF16),
            jax.ShapeDtypeStruct((SPAN, total, doubled), BF16),
            jax.ShapeDtypeStruct((SPAN, total, doubled), BF16),
        ),
        in_specs=[VMEM] * len(every),
        out_specs=(VMEM, VMEM, VMEM),
        scratch_shapes=[pltpu.VMEM((2, boxes * (total + 1) + total, points), F32)],
        compiler_params=params(6),
        name="pack",
    )(*every)
    before = lax.ppermute(tail, "leaf", [(i, (i + 1) % leaves) for i in range(leaves)])
    after = lax.ppermute(head, "leaf", [((i + 1) % leaves, i) for i in range(leaves)])

    near_ids = neighbours.T
    inner = boxes - 2 * SPAN
    inner_rows = pl.pallas_call(
        inner_kernel,
        out_shape=jax.ShapeDtypeStruct((parts, inner, angles * 2 * owned), BF16),
        in_specs=[SMEM, VMEM, VMEM],
        out_specs=VMEM,
        scratch_shapes=[pltpu.VMEM((parts * (inner + 1) + parts, angles * 2 * owned), F32)],
        compiler_params=params(4),
        cost_estimate=pl.CostEstimate(flops=2**31, bytes_accessed=2**21, transcendentals=0),
        name="inner",
    )(near_ids, own, near_blocks)
    rows = pl.pallas_call(
        outer_kernel,
        out_shape=jax.ShapeDtypeStruct((parts, boxes, angles * 2 * owned), BF16),
        in_specs=[SMEM] + [VMEM] * 5,
        out_specs=VMEM,
        scratch_shapes=[
            pltpu.VMEM((6 * SPAN, total, doubled), BF16),
            pltpu.VMEM((parts * (boxes + 1) + parts, angles * 2 * owned), F32),
        ],
        compiler_params=params(6),
        cost_estimate=pl.CostEstimate(flops=2**36, bytes_accessed=2**21, transcendentals=0),
        name="outer",
    )(near_ids, own, before, after, inner_rows, near_blocks)
    near = lax.all_to_all(rows, "rhs", split_axis=0, concat_axis=0, tiled=True)

    turned = pl.pallas_call(
        turn_kernel,
        out_shape=jax.ShapeDtypeStruct((kernel_count, wide, wide), BF16),
        in_specs=[VMEM],
        out_specs=VMEM,
        scratch_shapes=[pltpu.VMEM((kernel_count * PITCH, wide), F32)],
        compiler_params=params(12),
        cost_estimate=pl.CostEstimate(flops=2**31, bytes_accessed=6 * 2**20, transcendentals=0),
        name="turn",
    )(kernels_two)

    far = pl.pallas_call(
        far_kernel,
        out_shape=jax.ShapeDtypeStruct((2, angles * boxes, points), F32),
        in_specs=[ANY, ANY, ANY, ANY],
        out_specs=VMEM,
        scratch_shapes=[
            pltpu.VMEM((boxes, leaves * boxes), jnp.int32),
            pltpu.VMEM((leaves * boxes, angles * wide), BF16),
            pltpu.VMEM((kernel_count, wide, wide), BF16),
            pltpu.VMEM((boxes, 2, rank, points), BF16),
            pltpu.VMEM((boxes, leaves * boxes), BF16),
            pltpu.VMEM((angles * boxes, wide), F32),
            pltpu.SemaphoreType.DMA((kernel_count // CHUNK + 3,)),
        ],
        compiler_params=params(60),
        cost_estimate=pl.CostEstimate(flops=2**33, bytes_accessed=8 * 2**20, transcendentals=0),
        name="far",
    )(target_maps.T, incoming.reshape(leaves * boxes, angles * wide), turned, lines(target_bases))

    return pl.pallas_call(
        finish_kernel,
        out_shape=jax.ShapeDtypeStruct((angles, boxes, doubled), F32),
        in_specs=[SMEM, VMEM, VMEM],
        out_specs=VMEM,
        compiler_params=params(4),
        name="finish",
    )(counts, near, far)


def solution(mesh):
    placed = (
        P("rhs", "leaf", None),
        P("leaf"),
        P("leaf", None),
        P("leaf", None),
        P(None, "leaf"),
        P("leaf", None, None, None),
        P(),
        P(),
        P("leaf", None, None, None),
        P("leaf", None, None, "rhs", None),
    )
    return jax.shard_map(
        shards, mesh=mesh, in_specs=placed, out_specs=P("rhs", "leaf", None), check_vma=False
    )
```

```python
import jax
import jax.numpy as jnp
from jax import lax
from jax.experimental import pallas as pl
from jax.experimental.pallas import tpu as pltpu
from jax.sharding import PartitionSpec as P

SPAN = 8
PITCH = 129
F32 = jnp.float32
BF16 = jnp.bfloat16
VMEM = pl.BlockSpec(memory_space=pltpu.VMEM)
SMEM = pl.BlockSpec(memory_space=pltpu.SMEM)
ANY = pl.BlockSpec(memory_space=pl.ANY)
NT = (((1,), (1,)), ((), ()))


def params(mib):
    return pltpu.CompilerParams(vmem_limit_bytes=mib * 2**20)


def live_lanes(counts_ref, boxes, points):
    row = lax.broadcasted_iota(jnp.int32, (boxes, points), 0)
    limit = jnp.zeros((boxes, points), jnp.int32)
    for box in range(boxes):
        limit = jnp.where(row == box, counts_ref[box], limit)
    lane = lax.broadcasted_iota(jnp.int32, (boxes, points), 1)
    return lane < limit


def beside(*parts):
    return jnp.concatenate(parts, axis=1)


def above(*parts):
    return jnp.concatenate(parts, axis=0)


def turn_kernels(kernels_ref, turned, first, count):
    _, rank, _, kernel_count = kernels_ref.shape

    def one(step, _):
        r = first + step
        real, imag = kernels_ref[0, r], kernels_ref[1, r]
        turned[pl.ds(r, kernel_count, stride=PITCH), :] = above(real, imag).T.astype(F32)
        turned[pl.ds(rank + r, kernel_count, stride=PITCH), :] = above(-imag, real).T.astype(F32)
        return 0

    lax.fori_loop(0, count, one, 0, unroll=16)


def lift_kernel(
    counts_hbm,
    maps_hbm,
    currents_hbm,
    bases_hbm,
    kernels_hbm,
    out_hbm,
    counts_ref,
    maps_ref,
    currents_ref,
    bases_ref,
    kernels_ref,
    out_ref,
    rows,
    raws,
    turned,
    lifted,
    staged,
    arrived,
    sent,
):
    quarter = kernels_ref.shape[1] // 4

    def load_kernels(i):
        part = pl.ds(i * quarter, quarter)
        return pltpu.make_async_copy(kernels_hbm.at[:, part], kernels_ref.at[:, part], arrived.at[i])

    load_currents = pltpu.make_async_copy(currents_hbm, currents_ref, arrived.at[4])
    load_counts = pltpu.make_async_copy(counts_hbm, counts_ref, arrived.at[7])
    load_bases = pltpu.make_async_copy(bases_hbm, bases_ref, arrived.at[5])
    load_maps = pltpu.make_async_copy(maps_hbm, maps_ref, arrived.at[6])
    for i in range(4):
        load_kernels(i).start()
    load_currents.start()
    load_counts.start()
    load_bases.start()
    load_maps.start()
    for i in range(4):
        load_kernels(i).wait()
        turn_kernels(kernels_ref, turned, i * quarter, quarter)
    load_currents.wait()
    load_counts.wait()
    angles, boxes, doubled = currents_ref.shape
    points = doubled // 2
    _, rank, _, kernel_count = kernels_ref.shape
    groups = out_ref.shape[0]
    wide = 2 * rank
    each = 2 * angles
    live = live_lanes(counts_ref, boxes, points)
    for a in range(angles):
        for c in range(2):
            found = currents_ref[a, :, c * points : (c + 1) * points].astype(F32)
            rows[pl.ds(c * angles + a, boxes, stride=each), :] = jnp.where(live, found, 0.0)
    load_bases.wait()
    for box in range(boxes):
        x = rows[each * box : each * (box + 1), :].astype(BF16)
        raws[each * box : each * (box + 1), :] = lax.dot_general(
            x, above(bases_ref[box, 0], bases_ref[box, 1]), NT, preferred_element_type=F32
        )
    raw = raws[...].reshape(boxes, 2, angles, wide)
    crossed = pltpu.roll(raw[:, 1].reshape(boxes * angles, wide), rank, 1)
    lane = lax.broadcasted_iota(jnp.int32, crossed.shape, 1)
    straight = raw[:, 0].reshape(boxes * angles, wide)
    coef = (straight + jnp.where(lane < rank, -crossed, crossed)).astype(BF16)

    def pair(step, _):
        k = 2 * step
        weights = beside(turned[pl.ds(k * PITCH, wide), :], turned[pl.ds((k + 1) * PITCH, wide), :])
        both = jnp.dot(coef, weights.astype(BF16), preferred_element_type=F32)
        lifted[k] = both[:, :wide]
        lifted[k + 1] = both[:, wide:]
        return 0

    lax.fori_loop(0, kernel_count // 2, pair, 0, unroll=True)
    pitch = boxes + 1
    load_maps.wait()

    def one_group(g, slot):
        for box in range(boxes):
            k = maps_ref[box, g]
            staged[slot, pl.ds(box, angles, stride=pitch), :] = lifted[
                k, angles * box : angles * (box + 1), :
            ]
        for a in range(angles):
            out_ref[g, :, a * wide : (a + 1) * wide] = staged[
                slot, a * pitch : a * pitch + boxes, :
            ].astype(BF16)

    def send(step):
        part = pl.ds(step * 4, 4)
        return pltpu.make_async_copy(out_ref.at[part], out_hbm.at[part], sent.at[step])

    def four_groups(step, _):
        for i in range(4):
            one_group(4 * step + i, i)
        send(step).start()
        return 0

    lax.fori_loop(0, groups // 4, four_groups, 0)
    for step in range(groups // 4):
        send(step).wait()


def pack_kernel(counts_ref, *refs):
    every, (out_ref, head_ref, tail_ref, spread) = refs[:7], refs[-4:]
    angles, boxes, doubled = every[0].shape
    points = doubled // 2
    total = out_ref.shape[1]
    parts = total // angles
    pitch = total + 1
    live = live_lanes(counts_ref, boxes, points)
    me = lax.axis_index("rhs")
    back = 0
    for ref in every:
        for group in range(ref.shape[0] // angles):
            z = lax.rem(me + parts - back, parts)
            back += 1
            for a in range(angles):
                for c in range(2):
                    found = ref[group * angles + a, :, c * points : (c + 1) * points].astype(F32)
                    spread[c, pl.ds(a * parts + z, boxes, stride=pitch), :] = jnp.where(live, found, 0.0)
    for box in range(boxes):
        for c in range(2):
            lanes = slice(c * points, (c + 1) * points)
            rows = spread[c, box * pitch : box * pitch + total, :].astype(BF16)
            out_ref[box, :, lanes] = rows
            if box < SPAN:
                head_ref[box, :, lanes] = rows
            if box >= boxes - SPAN:
                tail_ref[box - (boxes - SPAN), :, lanes] = rows


def near_rows(sources, ids, blocks_ref, t, total, angles):
    nearby, _, owned, points = blocks_ref.shape[1:]
    parts = total // angles
    held, weights = [], []
    for n in range(nearby):
        held.append(sources[ids[n]])
        real, imag = blocks_ref[t, n, 0], blocks_ref[t, n, 1]
        weights.append(above(beside(real, -imag), beside(imag, real)))
    summed = lax.dot_general(beside(*held), beside(*weights), NT, preferred_element_type=F32)
    return beside(*[summed[a * parts : (a + 1) * parts] for a in range(angles)])


def inner_kernel(neighbours_ref, own_ref, blocks_ref, out_ref, rows):
    boxes, total, _ = own_ref.shape
    parts, inner, lanes = out_ref.shape
    angles = total // parts
    pitch = inner + 1

    def target(step, _):
        t = SPAN + step
        ids = [t + neighbours_ref[n, t] - neighbours_ref[0, t] for n in range(blocks_ref.shape[1])]
        rows[pl.ds(step, parts, stride=pitch), :] = near_rows(own_ref, ids, blocks_ref, t, total, angles)
        return 0

    lax.fori_loop(0, inner, target, 0, unroll=True)
    for z in range(parts):
        out_ref[z] = rows[z * pitch : z * pitch + inner, :].astype(BF16)


def outer_kernel(neighbours_ref, own_ref, before_ref, after_ref, inner_ref, blocks_ref, out_ref, window, rows):
    boxes, total, _ = own_ref.shape
    parts, _, lanes = out_ref.shape
    angles = total // parts
    pitch = boxes + 1
    window[:SPAN] = before_ref[...]
    window[SPAN : 3 * SPAN] = own_ref[: 2 * SPAN]
    window[3 * SPAN : 5 * SPAN] = own_ref[boxes - 2 * SPAN :]
    window[5 * SPAN :] = after_ref[...]

    def target(step, _):
        late = step // SPAN
        t = step + late * (boxes - 2 * SPAN)
        base = step + SPAN + late * 2 * SPAN - neighbours_ref[0, t]
        ids = [base + neighbours_ref[n, t] for n in range(blocks_ref.shape[1])]
        rows[pl.ds(t, parts, stride=pitch), :] = near_rows(window, ids, blocks_ref, t, total, angles)
        return 0

    lax.fori_loop(0, 2 * SPAN, target, 0, unroll=True)
    for z in range(parts):
        out_ref[z, :SPAN] = rows[z * pitch : z * pitch + SPAN, :].astype(BF16)
        out_ref[z, SPAN : boxes - SPAN] = inner_ref[z]
        out_ref[z, boxes - SPAN :] = rows[z * pitch + boxes - SPAN : z * pitch + boxes, :].astype(BF16)


def turn_kernel(kernels_ref, out_ref, turned):
    turn_kernels(kernels_ref, turned, 0, kernels_ref.shape[1])
    wide = out_ref.shape[1]

    def one(k, _):
        out_ref[k] = turned[pl.ds(k * PITCH, wide), :].astype(BF16)
        return 0

    lax.fori_loop(0, out_ref.shape[0], one, 0, unroll=32)


CHUNK = 32


def far_kernel(
    maps_hbm,
    pieces_hbm,
    kernels_hbm,
    bases_hbm,
    out_ref,
    maps_ref,
    pieces_ref,
    kernels_ref,
    bases_ref,
    table,
    total_ref,
    arrived,
):
    sources, lanes = pieces_hbm.shape
    kernel_count, wide, _ = kernels_hbm.shape
    boxes, _, _, points = bases_hbm.shape
    angles = lanes // wide
    chunks = kernel_count // CHUNK

    def load_kernels(step):
        part = pl.ds(step * CHUNK, CHUNK)
        return pltpu.make_async_copy(kernels_hbm.at[part], kernels_ref.at[part], arrived.at[step])

    load_bases = pltpu.make_async_copy(bases_hbm, bases_ref, arrived.at[chunks])
    load_maps = pltpu.make_async_copy(maps_hbm, maps_ref, arrived.at[chunks + 1])
    load_pieces = pltpu.make_async_copy(pieces_hbm, pieces_ref, arrived.at[chunks + 2])
    load_maps.start()
    load_pieces.start()
    for step in range(chunks):
        load_kernels(step).start()
    load_bases.start()
    load_maps.wait()
    table[...] = maps_ref[...].astype(F32).astype(BF16)
    one, zero = jnp.ones((), BF16), jnp.zeros((), BF16)
    load_pieces.wait()
    total = None
    for step in range(chunks):
        first = step * CHUNK
        maps = table[...]
        chosen = above(*[jnp.where(maps == jnp.asarray(first + i, BF16), one, zero) for i in range(CHUNK)])
        summed = jnp.dot(chosen, pieces_ref[...], preferred_element_type=F32)
        load_kernels(step).wait()
        xs = [
            above(
                *[summed[i * boxes : (i + 1) * boxes, a * wide : (a + 1) * wide] for a in range(angles)]
            ).astype(BF16)
            for i in range(CHUNK)
        ]
        weights = kernels_ref[first : first + CHUNK].reshape(CHUNK * wide, wide)
        add = jnp.dot(beside(*xs), weights, preferred_element_type=F32)
        total = add if total is None else total + add
    total_ref[...] = total
    load_bases.wait()
    for t in range(boxes):
        x = total_ref[pl.ds(t, angles, stride=boxes), :]
        high = x.astype(BF16).astype(F32)
        both = above(high, x - high).astype(BF16)
        real, imag = bases_ref[t, 0], bases_ref[t, 1]
        weights = beside(above(real, -imag), above(imag, real))
        far = jnp.dot(both, weights, preferred_element_type=F32)
        far = far[:angles] + far[angles:]
        for c in range(2):
            out_ref[c, pl.ds(t, angles, stride=boxes), :] = far[:, c * points : (c + 1) * points]


def finish_kernel(counts_ref, near_ref, far_ref, out_ref):
    parts, boxes, lanes = near_ref.shape
    angles, _, doubled = out_ref.shape
    points = doubled // 2
    owned = points // parts
    live = live_lanes(counts_ref, boxes, points)
    block = lax.broadcasted_iota(jnp.int32, (boxes, points), 1) // owned
    near = [near_ref[z].astype(F32) for z in range(parts)]
    for a in range(angles):
        for c in range(2):
            place = (a * 2 + c) * owned
            joined = jnp.zeros((boxes, points), F32)
            for z in range(parts):
                shift = (z * owned - place) % lanes
                moved = near[z] if shift == 0 else pltpu.roll(near[z], shift, 1)
                joined = jnp.where(block == z, moved, joined)
            lanes_out = slice(c * points, (c + 1) * points)
            far = far_ref[c, a * boxes : (a + 1) * boxes, :]
            out_ref[a, :, lanes_out] = jnp.where(live, joined + far, 0.0)


def shards(
    currents,
    counts,
    neighbours,
    source_maps,
    target_maps,
    source_bases,
    level_one,
    level_two,
    target_bases,
    near_blocks,
):
    angles, boxes, doubled = currents.shape
    points = doubled // 2
    kernel_count, _, rank, _ = level_one.shape
    wide = 2 * rank
    leaves, parts = lax.axis_size("leaf"), lax.axis_size("rhs")
    owned = near_blocks.shape[3]

    lines = lambda x: jnp.swapaxes(x, -1, -2)
    kernels_one = level_one.transpose(1, 2, 3, 0)
    kernels_two = level_two.transpose(1, 2, 3, 0)

    def passed(x, steps):
        return lax.ppermute(x, "rhs", [(i, (i + steps) % parts) for i in range(parts)])

    back1, ahead1 = passed(currents, 1), passed(currents, -1)
    back2, ahead2 = passed(currents, 2), passed(currents, -2)
    back34 = passed(jnp.concatenate([back1, back2], axis=0), 2)
    ahead3 = passed(ahead1, -2)
    every = (currents, back1, back2, back34, ahead3, ahead2, ahead1)

    pieces = pl.pallas_call(
        lift_kernel,
        out_shape=jax.ShapeDtypeStruct((leaves, boxes, angles * wide), BF16),
        in_specs=[ANY] * 5,
        out_specs=ANY,
        scratch_shapes=[
            pltpu.SMEM((boxes,), jnp.int32),
            pltpu.SMEM((boxes, leaves), jnp.int32),
            pltpu.VMEM((angles, boxes, doubled), BF16),
            pltpu.VMEM((boxes, 2, rank, points), BF16),
            pltpu.VMEM((2, rank, rank, kernel_count), BF16),
            pltpu.VMEM((leaves, boxes, angles * wide), BF16),
            pltpu.VMEM((boxes * 2 * angles, points), F32),
            pltpu.VMEM((boxes * 2 * angles, wide), F32),
            pltpu.VMEM((kernel_count * PITCH, wide), F32),
            pltpu.VMEM((kernel_count, boxes * angles, wide), F32),
            pltpu.VMEM((4, angles * (boxes + 1) + angles, wide), F32),
            pltpu.SemaphoreType.DMA((8,)),
            pltpu.SemaphoreType.DMA((leaves // 4,)),
        ],
        compiler_params=params(60),
        cost_estimate=pl.CostEstimate(flops=2**33, bytes_accessed=8 * 2**20, transcendentals=0),
        name="lift",
    )(counts, source_maps, currents, lines(source_bases), kernels_one)
    incoming = lax.all_to_all(pieces, "leaf", split_axis=0, concat_axis=0, tiled=True)

    total = parts * angles
    own, head, tail = pl.pallas_call(
        pack_kernel,
        out_shape=(
            jax.ShapeDtypeStruct((boxes, total, doubled), BF16),
            jax.ShapeDtypeStruct((SPAN, total, doubled), BF16),
            jax.ShapeDtypeStruct((SPAN, total, doubled), BF16),
        ),
        in_specs=[SMEM] + [VMEM] * len(every),
        out_specs=(VMEM, VMEM, VMEM),
        scratch_shapes=[pltpu.VMEM((2, boxes * (total + 1) + total, points), F32)],
        compiler_params=params(6),
        name="pack",
    )(counts, *every)
    before = lax.ppermute(tail, "leaf", [(i, (i + 1) % leaves) for i in range(leaves)])
    after = lax.ppermute(head, "leaf", [((i + 1) % leaves, i) for i in range(leaves)])

    near_ids = neighbours.T
    inner = boxes - 2 * SPAN
    inner_rows = pl.pallas_call(
        inner_kernel,
        out_shape=jax.ShapeDtypeStruct((parts, inner, angles * 2 * owned), BF16),
        in_specs=[SMEM, VMEM, VMEM],
        out_specs=VMEM,
        scratch_shapes=[pltpu.VMEM((parts * (inner + 1) + parts, angles * 2 * owned), F32)],
        compiler_params=params(4),
        cost_estimate=pl.CostEstimate(flops=2**31, bytes_accessed=2**21, transcendentals=0),
        name="inner",
    )(near_ids, own, near_blocks)
    rows = pl.pallas_call(
        outer_kernel,
        out_shape=jax.ShapeDtypeStruct((parts, boxes, angles * 2 * owned), BF16),
        in_specs=[SMEM] + [VMEM] * 5,
        out_specs=VMEM,
        scratch_shapes=[
            pltpu.VMEM((6 * SPAN, total, doubled), BF16),
            pltpu.VMEM((parts * (boxes + 1) + parts, angles * 2 * owned), F32),
        ],
        compiler_params=params(6),
        cost_estimate=pl.CostEstimate(flops=2**36, bytes_accessed=2**21, transcendentals=0),
        name="outer",
    )(near_ids, own, before, after, inner_rows, near_blocks)
    near = lax.all_to_all(rows, "rhs", split_axis=0, concat_axis=0, tiled=True)

    turned = pl.pallas_call(
        turn_kernel,
        out_shape=jax.ShapeDtypeStruct((kernel_count, wide, wide), BF16),
        in_specs=[VMEM],
        out_specs=VMEM,
        scratch_shapes=[pltpu.VMEM((kernel_count * PITCH, wide), F32)],
        compiler_params=params(12),
        cost_estimate=pl.CostEstimate(flops=2**31, bytes_accessed=6 * 2**20, transcendentals=0),
        name="turn",
    )(kernels_two)

    far = pl.pallas_call(
        far_kernel,
        out_shape=jax.ShapeDtypeStruct((2, angles * boxes, points), F32),
        in_specs=[ANY, ANY, ANY, ANY],
        out_specs=VMEM,
        scratch_shapes=[
            pltpu.VMEM((boxes, leaves * boxes), jnp.int32),
            pltpu.VMEM((leaves * boxes, angles * wide), BF16),
            pltpu.VMEM((kernel_count, wide, wide), BF16),
            pltpu.VMEM((boxes, 2, rank, points), BF16),
            pltpu.VMEM((boxes, leaves * boxes), BF16),
            pltpu.VMEM((angles * boxes, wide), F32),
            pltpu.SemaphoreType.DMA((kernel_count // CHUNK + 3,)),
        ],
        compiler_params=params(60),
        cost_estimate=pl.CostEstimate(flops=2**33, bytes_accessed=8 * 2**20, transcendentals=0),
        name="far",
    )(target_maps.T, incoming.reshape(leaves * boxes, angles * wide), turned, lines(target_bases))

    return pl.pallas_call(
        finish_kernel,
        out_shape=jax.ShapeDtypeStruct((angles, boxes, doubled), F32),
        in_specs=[SMEM, VMEM, VMEM],
        out_specs=VMEM,
        compiler_params=params(4),
        name="finish",
    )(counts, near, far)


def solution(mesh):
    placed = (
        P("rhs", "leaf", None),
        P("leaf"),
        P("leaf", None),
        P("leaf", None),
        P(None, "leaf"),
        P("leaf", None, None, None),
        P(),
        P(),
        P("leaf", None, None, None),
        P("leaf", None, None, "rhs", None),
    )
    return jax.shard_map(
        shards, mesh=mesh, in_specs=placed, out_specs=P("rhs", "leaf", None), check_vma=False
    )
```

```python
import jax
import jax.numpy as jnp
from jax import lax
from jax.experimental import pallas as pl
from jax.experimental.pallas import tpu as pltpu
from jax.sharding import PartitionSpec as P

SPAN = 8
PITCH = 129
F32 = jnp.float32
BF16 = jnp.bfloat16
VMEM = pl.BlockSpec(memory_space=pltpu.VMEM)
SMEM = pl.BlockSpec(memory_space=pltpu.SMEM)
ANY = pl.BlockSpec(memory_space=pl.ANY)
NT = (((1,), (1,)), ((), ()))


def params(mib):
    return pltpu.CompilerParams(vmem_limit_bytes=mib * 2**20)


def live_lanes(counts_ref, boxes, points):
    row = lax.broadcasted_iota(jnp.int32, (boxes, points), 0)
    limit = jnp.zeros((boxes, points), jnp.int32)
    for box in range(boxes):
        limit = jnp.where(row == box, counts_ref[box], limit)
    lane = lax.broadcasted_iota(jnp.int32, (boxes, points), 1)
    return lane < limit


def beside(*parts):
    return jnp.concatenate(parts, axis=1)


def above(*parts):
    return jnp.concatenate(parts, axis=0)


def turn_kernels(kernels_ref, turned, first, count):
    _, rank, _, kernel_count = kernels_ref.shape

    def one(step, _):
        r = first + step
        real, imag = kernels_ref[0, r], kernels_ref[1, r]
        turned[pl.ds(r, kernel_count, stride=PITCH), :] = above(real, imag).T.astype(F32)
        turned[pl.ds(rank + r, kernel_count, stride=PITCH), :] = above(-imag, real).T.astype(F32)
        return 0

    lax.fori_loop(0, count, one, 0, unroll=16)


def lift_kernel(
    counts_hbm,
    maps_hbm,
    currents_hbm,
    bases_hbm,
    kernels_hbm,
    out_hbm,
    counts_ref,
    maps_ref,
    currents_ref,
    bases_ref,
    kernels_ref,
    out_ref,
    rows,
    raws,
    turned,
    lifted,
    staged,
    arrived,
    sent,
):
    quarter = kernels_ref.shape[1] // 4

    def load_kernels(i):
        part = pl.ds(i * quarter, quarter)
        return pltpu.make_async_copy(kernels_hbm.at[:, part], kernels_ref.at[:, part], arrived.at[i])

    load_currents = pltpu.make_async_copy(currents_hbm, currents_ref, arrived.at[4])
    load_counts = pltpu.make_async_copy(counts_hbm, counts_ref, arrived.at[7])
    load_bases = pltpu.make_async_copy(bases_hbm, bases_ref, arrived.at[5])
    load_maps = pltpu.make_async_copy(maps_hbm, maps_ref, arrived.at[6])
    for i in range(4):
        load_kernels(i).start()
    load_currents.start()
    load_counts.start()
    load_bases.start()
    load_maps.start()
    for i in range(4):
        load_kernels(i).wait()
        turn_kernels(kernels_ref, turned, i * quarter, quarter)
    load_currents.wait()
    load_counts.wait()
    angles, boxes, doubled = currents_ref.shape
    points = doubled // 2
    _, rank, _, kernel_count = kernels_ref.shape
    groups = out_ref.shape[0]
    wide = 2 * rank
    each = 2 * angles
    live = live_lanes(counts_ref, boxes, points)
    for a in range(angles):
        for c in range(2):
            found = currents_ref[a, :, c * points : (c + 1) * points].astype(F32)
            rows[pl.ds(c * angles + a, boxes, stride=each), :] = jnp.where(live, found, 0.0)
    load_bases.wait()
    for box in range(boxes):
        x = rows[each * box : each * (box + 1), :].astype(BF16)
        raws[each * box : each * (box + 1), :] = lax.dot_general(
            x, above(bases_ref[box, 0], bases_ref[box, 1]), NT, preferred_element_type=F32
        )
    raw = raws[...].reshape(boxes, 2, angles, wide)
    crossed = pltpu.roll(raw[:, 1].reshape(boxes * angles, wide), rank, 1)
    lane = lax.broadcasted_iota(jnp.int32, crossed.shape, 1)
    straight = raw[:, 0].reshape(boxes * angles, wide)
    coef = (straight + jnp.where(lane < rank, -crossed, crossed)).astype(BF16)

    def pair(step, _):
        k = 2 * step
        weights = beside(turned[pl.ds(k * PITCH, wide), :], turned[pl.ds((k + 1) * PITCH, wide), :])
        both = jnp.dot(coef, weights.astype(BF16), preferred_element_type=F32)
        lifted[k] = both[:, :wide]
        lifted[k + 1] = both[:, wide:]
        return 0

    lax.fori_loop(0, kernel_count // 2, pair, 0, unroll=True)
    pitch = boxes + 1
    load_maps.wait()

    def one_group(g, slot):
        for box in range(boxes):
            k = maps_ref[box, g]
            staged[slot, pl.ds(box, angles, stride=pitch), :] = lifted[
                k, angles * box : angles * (box + 1), :
            ]
        for a in range(angles):
            out_ref[g, :, a * wide : (a + 1) * wide] = staged[
                slot, a * pitch : a * pitch + boxes, :
            ].astype(BF16)

    def send(step):
        part = pl.ds(step * 4, 4)
        return pltpu.make_async_copy(out_ref.at[part], out_hbm.at[part], sent.at[step])

    def four_groups(step, _):
        for i in range(4):
            one_group(4 * step + i, i)
        send(step).start()
        return 0

    lax.fori_loop(0, groups // 4, four_groups, 0)
    for step in range(groups // 4):
        send(step).wait()


def pack_kernel(counts_ref, *refs):
    every, (out_ref, head_ref, tail_ref, spread) = refs[:7], refs[-4:]
    angles, boxes, doubled = every[0].shape
    points = doubled // 2
    total = out_ref.shape[1]
    parts = total // angles
    pitch = total + 1
    live = live_lanes(counts_ref, boxes, points)
    me = lax.axis_index("rhs")
    back = 0
    for ref in every:
        for group in range(ref.shape[0] // angles):
            z = lax.rem(me + parts - back, parts)
            back += 1
            for a in range(angles):
                for c in range(2):
                    found = ref[group * angles + a, :, c * points : (c + 1) * points].astype(F32)
                    spread[c, pl.ds(a * parts + z, boxes, stride=pitch), :] = jnp.where(live, found, 0.0)
    for box in range(boxes):
        for c in range(2):
            lanes = slice(c * points, (c + 1) * points)
            rows = spread[c, box * pitch : box * pitch + total, :].astype(BF16)
            out_ref[box, :, lanes] = rows
            if box < SPAN:
                head_ref[box, :, lanes] = rows
            if box >= boxes - SPAN:
                tail_ref[box - (boxes - SPAN), :, lanes] = rows


def near_rows(sources, ids, blocks_ref, t, total, angles):
    nearby, _, owned, points = blocks_ref.shape[1:]
    parts = total // angles
    held, weights = [], []
    for n in range(nearby):
        held.append(sources[ids[n]])
        real, imag = blocks_ref[t, n, 0], blocks_ref[t, n, 1]
        weights.append(above(beside(real, -imag), beside(imag, real)))
    summed = lax.dot_general(beside(*held), beside(*weights), NT, preferred_element_type=F32)
    return beside(*[summed[a * parts : (a + 1) * parts] for a in range(angles)])


def inner_kernel(neighbours_ref, own_ref, blocks_ref, out_ref, rows):
    boxes, total, _ = own_ref.shape
    parts, inner, lanes = out_ref.shape
    angles = total // parts
    pitch = inner + 1

    def target(step, _):
        t = SPAN + step
        ids = [t + neighbours_ref[n, t] - neighbours_ref[0, t] for n in range(blocks_ref.shape[1])]
        rows[pl.ds(step, parts, stride=pitch), :] = near_rows(own_ref, ids, blocks_ref, t, total, angles)
        return 0

    lax.fori_loop(0, inner, target, 0, unroll=True)
    for z in range(parts):
        out_ref[z] = rows[z * pitch : z * pitch + inner, :].astype(BF16)


def outer_kernel(neighbours_ref, own_ref, before_ref, after_ref, inner_ref, blocks_ref, out_ref, window, rows):
    boxes, total, _ = own_ref.shape
    parts, _, lanes = out_ref.shape
    angles = total // parts
    pitch = boxes + 1
    window[:SPAN] = before_ref[...]
    window[SPAN : 3 * SPAN] = own_ref[: 2 * SPAN]
    window[3 * SPAN : 5 * SPAN] = own_ref[boxes - 2 * SPAN :]
    window[5 * SPAN :] = after_ref[...]

    def target(step, _):
        late = step // SPAN
        t = step + late * (boxes - 2 * SPAN)
        base = step + SPAN + late * 2 * SPAN - neighbours_ref[0, t]
        ids = [base + neighbours_ref[n, t] for n in range(blocks_ref.shape[1])]
        rows[pl.ds(t, parts, stride=pitch), :] = near_rows(window, ids, blocks_ref, t, total, angles)
        return 0

    lax.fori_loop(0, 2 * SPAN, target, 0, unroll=True)
    for z in range(parts):
        out_ref[z, :SPAN] = rows[z * pitch : z * pitch + SPAN, :].astype(BF16)
        out_ref[z, SPAN : boxes - SPAN] = inner_ref[z]
        out_ref[z, boxes - SPAN :] = rows[z * pitch + boxes - SPAN : z * pitch + boxes, :].astype(BF16)


def turn_kernel(kernels_ref, out_ref, turned):
    turn_kernels(kernels_ref, turned, 0, kernels_ref.shape[1])
    wide = out_ref.shape[1]

    def one(k, _):
        out_ref[k] = turned[pl.ds(k * PITCH, wide), :].astype(BF16)
        return 0

    lax.fori_loop(0, out_ref.shape[0], one, 0, unroll=32)


CHUNK = 32


def far_kernel(
    maps_hbm,
    pieces_hbm,
    kernels_hbm,
    bases_hbm,
    out_ref,
    maps_ref,
    pieces_ref,
    kernels_ref,
    bases_ref,
    table,
    total_ref,
    arrived,
):
    sources, lanes = pieces_hbm.shape
    kernel_count, wide, _ = kernels_hbm.shape
    boxes, _, _, points = bases_hbm.shape
    angles = lanes // wide
    chunks = kernel_count // CHUNK

    def load_kernels(step):
        part = pl.ds(step * CHUNK, CHUNK)
        return pltpu.make_async_copy(kernels_hbm.at[part], kernels_ref.at[part], arrived.at[step])

    load_bases = pltpu.make_async_copy(bases_hbm, bases_ref, arrived.at[chunks])
    load_maps = pltpu.make_async_copy(maps_hbm, maps_ref, arrived.at[chunks + 1])
    load_pieces = pltpu.make_async_copy(pieces_hbm, pieces_ref, arrived.at[chunks + 2])
    load_maps.start()
    load_pieces.start()
    for step in range(chunks):
        load_kernels(step).start()
    load_bases.start()
    load_maps.wait()
    table[...] = maps_ref[...].astype(F32).astype(BF16)
    one, zero = jnp.ones((), BF16), jnp.zeros((), BF16)
    load_pieces.wait()
    total = None
    for step in range(chunks):
        first = step * CHUNK
        maps = table[...]
        chosen = above(*[jnp.where(maps == jnp.asarray(first + i, BF16), one, zero) for i in range(CHUNK)])
        summed = jnp.dot(chosen, pieces_ref[...], preferred_element_type=F32)
        load_kernels(step).wait()
        xs = [
            above(
                *[summed[i * boxes : (i + 1) * boxes, a * wide : (a + 1) * wide] for a in range(angles)]
            ).astype(BF16)
            for i in range(CHUNK)
        ]
        weights = kernels_ref[first : first + CHUNK].reshape(CHUNK * wide, wide)
        add = jnp.dot(beside(*xs), weights, preferred_element_type=F32)
        total = add if total is None else total + add
    total_ref[...] = total
    load_bases.wait()
    for t in range(boxes):
        x = total_ref[pl.ds(t, angles, stride=boxes), :]
        high = x.astype(BF16).astype(F32)
        both = above(high, x - high).astype(BF16)
        real, imag = bases_ref[t, 0], bases_ref[t, 1]
        weights = beside(above(real, -imag), above(imag, real))
        far = jnp.dot(both, weights, preferred_element_type=F32)
        far = far[:angles] + far[angles:]
        for c in range(2):
            out_ref[c, pl.ds(t, angles, stride=boxes), :] = far[:, c * points : (c + 1) * points]


def finish_kernel(counts_ref, near_ref, far_ref, out_ref):
    parts, boxes, lanes = near_ref.shape
    angles, _, doubled = out_ref.shape
    points = doubled // 2
    owned = points // parts
    live = live_lanes(counts_ref, boxes, points)
    block = lax.broadcasted_iota(jnp.int32, (boxes, points), 1) // owned
    near = [near_ref[z].astype(F32) for z in range(parts)]
    for a in range(angles):
        for c in range(2):
            place = (a * 2 + c) * owned
            joined = jnp.zeros((boxes, points), F32)
            for z in range(parts):
                shift = (z * owned - place) % lanes
                moved = near[z] if shift == 0 else pltpu.roll(near[z], shift, 1)
                joined = jnp.where(block == z, moved, joined)
            lanes_out = slice(c * points, (c + 1) * points)
            far = far_ref[c, a * boxes : (a + 1) * boxes, :]
            out_ref[a, :, lanes_out] = jnp.where(live, joined + far, 0.0)


def shards(
    currents,
    counts,
    neighbours,
    source_maps,
    target_maps,
    source_bases,
    level_one,
    level_two,
    target_bases,
    near_blocks,
):
    angles, boxes, doubled = currents.shape
    points = doubled // 2
    kernel_count, _, rank, _ = level_one.shape
    wide = 2 * rank
    leaves, parts = lax.axis_size("leaf"), lax.axis_size("rhs")
    owned = near_blocks.shape[3]

    lines = lambda x: jnp.swapaxes(x, -1, -2)
    kernels_one = level_one.transpose(1, 2, 3, 0)
    kernels_two = level_two.transpose(1, 2, 3, 0)

    def passed(x, steps):
        return lax.ppermute(x, "rhs", [(i, (i + steps) % parts) for i in range(parts)])

    back1, ahead1 = passed(currents, 1), passed(currents, -1)
    back2, ahead2 = passed(currents, 2), passed(currents, -2)
    back34 = passed(jnp.concatenate([back1, back2], axis=0), 2)
    ahead3 = passed(ahead1, -2)
    every = (currents, back1, back2, back34, ahead3, ahead2, ahead1)

    pieces = pl.pallas_call(
        lift_kernel,
        out_shape=jax.ShapeDtypeStruct((leaves, boxes, angles * wide), BF16),
        in_specs=[ANY] * 5,
        out_specs=ANY,
        scratch_shapes=[
            pltpu.SMEM((boxes,), jnp.int32),
            pltpu.SMEM((boxes, leaves), jnp.int32),
            pltpu.VMEM((angles, boxes, doubled), BF16),
            pltpu.VMEM((boxes, 2, rank, points), BF16),
            pltpu.VMEM((2, rank, rank, kernel_count), BF16),
            pltpu.VMEM((leaves, boxes, angles * wide), BF16),
            pltpu.VMEM((boxes * 2 * angles, points), F32),
            pltpu.VMEM((boxes * 2 * angles, wide), F32),
            pltpu.VMEM((kernel_count * PITCH, wide), F32),
            pltpu.VMEM((kernel_count, boxes * angles, wide), F32),
            pltpu.VMEM((4, angles * (boxes + 1) + angles, wide), F32),
            pltpu.SemaphoreType.DMA((8,)),
            pltpu.SemaphoreType.DMA((leaves // 4,)),
        ],
        compiler_params=params(60),
        cost_estimate=pl.CostEstimate(flops=2**33, bytes_accessed=8 * 2**20, transcendentals=0),
        name="lift",
    )(counts, source_maps, currents, lines(source_bases), kernels_one)
    incoming = lax.all_to_all(pieces, "leaf", split_axis=0, concat_axis=0, tiled=True)

    total = parts * angles
    own, head, tail = pl.pallas_call(
        pack_kernel,
        out_shape=(
            jax.ShapeDtypeStruct((boxes, total, doubled), BF16),
            jax.ShapeDtypeStruct((SPAN, total, doubled), BF16),
            jax.ShapeDtypeStruct((SPAN, total, doubled), BF16),
        ),
        in_specs=[SMEM] + [VMEM] * len(every),
        out_specs=(VMEM, VMEM, VMEM),
        scratch_shapes=[pltpu.VMEM((2, boxes * (total + 1) + total, points), F32)],
        compiler_params=params(6),
        name="pack",
    )(counts, *every)
    before = lax.ppermute(tail, "leaf", [(i, (i + 1) % leaves) for i in range(leaves)])
    after = lax.ppermute(head, "leaf", [((i + 1) % leaves, i) for i in range(leaves)])

    near_ids = neighbours.T
    inner = boxes - 2 * SPAN
    inner_rows = pl.pallas_call(
        inner_kernel,
        out_shape=jax.ShapeDtypeStruct((parts, inner, angles * 2 * owned), BF16),
        in_specs=[SMEM, VMEM, VMEM],
        out_specs=VMEM,
        scratch_shapes=[pltpu.VMEM((parts * (inner + 1) + parts, angles * 2 * owned), F32)],
        compiler_params=params(4),
        cost_estimate=pl.CostEstimate(flops=2**31, bytes_accessed=2**21, transcendentals=0),
        name="inner",
    )(near_ids, own, near_blocks)
    rows = pl.pallas_call(
        outer_kernel,
        out_shape=jax.ShapeDtypeStruct((parts, boxes, angles * 2 * owned), BF16),
        in_specs=[SMEM] + [VMEM] * 5,
        out_specs=VMEM,
        scratch_shapes=[
            pltpu.VMEM((6 * SPAN, total, doubled), BF16),
            pltpu.VMEM((parts * (boxes + 1) + parts, angles * 2 * owned), F32),
        ],
        compiler_params=params(6),
        cost_estimate=pl.CostEstimate(flops=2**36, bytes_accessed=2**21, transcendentals=0),
        name="outer",
    )(near_ids, own, before, after, inner_rows, near_blocks)
    near = lax.all_to_all(rows, "rhs", split_axis=0, concat_axis=0, tiled=True)

    turned = pl.pallas_call(
        turn_kernel,
        out_shape=jax.ShapeDtypeStruct((kernel_count, wide, wide), BF16),
        in_specs=[VMEM],
        out_specs=VMEM,
        scratch_shapes=[pltpu.VMEM((kernel_count * PITCH, wide), F32)],
        compiler_params=params(12),
        cost_estimate=pl.CostEstimate(flops=2**31, bytes_accessed=6 * 2**20, transcendentals=0),
        name="turn",
    )(kernels_two)

    far = pl.pallas_call(
        far_kernel,
        out_shape=jax.ShapeDtypeStruct((2, angles * boxes, points), F32),
        in_specs=[ANY, ANY, ANY, ANY],
        out_specs=VMEM,
        scratch_shapes=[
            pltpu.VMEM((boxes, leaves * boxes), jnp.int32),
            pltpu.VMEM((leaves * boxes, angles * wide), BF16),
            pltpu.VMEM((kernel_count, wide, wide), BF16),
            pltpu.VMEM((boxes, 2, rank, points), BF16),
            pltpu.VMEM((boxes, leaves * boxes), BF16),
            pltpu.VMEM((angles * boxes, wide), F32),
            pltpu.SemaphoreType.DMA((kernel_count // CHUNK + 3,)),
        ],
        compiler_params=params(48),
        cost_estimate=pl.CostEstimate(flops=2**33, bytes_accessed=8 * 2**20, transcendentals=0),
        name="far",
    )(target_maps.T, incoming.reshape(leaves * boxes, angles * wide), turned, lines(target_bases))

    return pl.pallas_call(
        finish_kernel,
        out_shape=jax.ShapeDtypeStruct((angles, boxes, doubled), F32),
        in_specs=[SMEM, VMEM, VMEM],
        out_specs=VMEM,
        compiler_params=params(4),
        name="finish",
    )(counts, near, far)


def solution(mesh):
    placed = (
        P("rhs", "leaf", None),
        P("leaf"),
        P("leaf", None),
        P("leaf", None),
        P(None, "leaf"),
        P("leaf", None, None, None),
        P(),
        P(),
        P("leaf", None, None, None),
        P("leaf", None, None, "rhs", None),
    )
    return jax.shard_map(
        shards, mesh=mesh, in_specs=placed, out_specs=P("rhs", "leaf", None), check_vma=False
    )
```
